32 devices in a mesh: group: 2 (over y), member: 4 (over z), strip: 2 (over x), sub: 2 (over core).
Axes of the slice: x: 2, y: 2, z: 4, core: 2. Of those that a mesh axis runs over, the one named last changes fastest.
Arguments:
- noisy: bfloat16 [8, 128, 128, 256], P(('group', 'member'), None, 'strip', 'sub'), parts along dimension 0, may hold values from -6 to 6
- condition: bfloat16 [24, 128, 256], P('group', ('strip', 'member'), 'sub'), parts along dimension 0, may hold values from -6 to 6
- levels: int32 [8], P(('group', 'member')), parts along dimension 0, may hold values from 0 to 17
- enc_w1: bfloat16 [9, 128, 12], replicated, may hold values from -0.625 to 0.625
- enc_b1: float32 [128], replicated, may hold values from -4 to 4
- enc_w2: bfloat16 [9, 128, 128], replicated, may hold values from -0.1875 to 0.1875
- enc_b2: float32 [128], replicated, may hold values from -4 to 4
- den_wa: bfloat16 [9, 128, 256], replicated, may hold values from -0.125 to 0.125
- den_ba: float32 [128], replicated, may hold values from -4 to 4
- noise_gain: float32 [128], replicated, may hold values from -6 to 6
- den_wb: bfloat16 [9, 128, 128], replicated, may hold values from -0.1875 to 0.1875
Outputs:
- denoised: bfloat16 [8, 128, 128, 256], P(('group', 'member'), None, 'strip', 'sub'), parts along dimension 0
The draws below stay inside these ranges and needn't reach their ends.
There are 2 independent parts, one for each index of `group`. The reference program is written for one: setup_inputs(seed, part) draws one part's arguments, and reference() takes and returns one part's arrays. A program takes and returns all parts, laid end to end along the dimension named above; an argument that names none is the same for every part. Nothing has to cross between parts.
All inputs are finite; a program needn't handle non-finite values.
Results may differ from the reference program's by a relative error of at most 0.0043.
The reference program's roundings to bfloat16 on the way (of `enc_first`, `features`, `joined` and `hidden`) count: a program that leaves them out, or rounds other values in their place, can miss the bound.
Values may be sent and summed in bfloat16 or wider, within the bound.
No kernel may reach another device: no remote copies, remote signals or barrier semaphores. Data moves between devices by JAX's collectives and lax.ppermute only.
A program may use at most 64 MiB of HBM per device.

```python
import jax
import jax.numpy as jnp
from jax import lax

C = 128
CIN = 12
LEVELS = 18
MEMBERS = 4
H = 128
W = 256


def set_ends(entries, key, low, largest):
    longest = entries.shape.index(max(entries.shape))
    spots = []
    for shift in (0, 1):
        where = [jax.random.randint(jax.random.fold_in(key, axis), (), 0, length) for axis, length in enumerate(entries.shape)]
        where[longest] = (where[longest] + shift) % entries.shape[longest]
        spots.append(tuple(where))
    return entries.at[spots[0]].set(low).at[spots[1]].set(largest)


def block_scale(rng, dims, split, smallest, largest):
    def one(axis_at, blocks):
        heights = jax.random.uniform(jax.random.fold_in(jax.random.fold_in(rng, 6), axis_at), (blocks,), jnp.float32, smallest / len(split), largest / len(split))
        return jnp.repeat(jnp.exp(heights), dims[axis_at] // blocks).reshape((-1,) + (1,) * (len(dims) - axis_at - 1))

    factor_of = one(*split[0])
    for cut in split[1:]:
        factor_of = factor_of * one(*cut)
    return factor_of


def scatter_about(own_key, dims, deviation, bound, pieces=(), held_as=jnp.bfloat16):
    drawn = deviation * jax.random.normal(own_key, dims, jnp.float32)
    if pieces:
        drawn = drawn * block_scale(own_key, dims, pieces, -0.22, 0.18)
    return jnp.clip(drawn, -bound, bound).astype(held_as)


def setup_inputs(seed: int = 0, part: int = 0) -> dict:
    key_list = jax.random.split(jax.random.key(seed), 12)
    part_splits = jax.random.split(jax.random.fold_in(key_list[11], part), 12)
    return {
        "noisy": scatter_about(part_splits[0], (MEMBERS, C, H, W), 1.0, 6.0, ((0, 4), (2, 2), (3, 2))),
        "condition": scatter_about(part_splits[1], (CIN, H, W), 1.0, 6.0, ((1, 8), (2, 2))),
        "levels": set_ends(jax.random.randint(part_splits[2], (MEMBERS,), 0, LEVELS), jax.random.fold_in(part_splits[2], 1), 0, LEVELS - 1).astype(jnp.int32),
        "enc_w1": scatter_about(key_list[3], (9, C, CIN), (9 * CIN) ** -0.5, 0.625),
        "enc_b1": scatter_about(key_list[4], (C,), 1.0, 4.0, (), jnp.float32),
        "enc_w2": scatter_about(key_list[5], (9, C, C), (9 * C) ** -0.5, 0.1875),
        "enc_b2": scatter_about(key_list[6], (C,), 1.0, 4.0, (), jnp.float32),
        "den_wa": scatter_about(key_list[7], (9, C, 2 * C), (18 * C) ** -0.5, 0.125),
        "den_ba": scatter_about(key_list[8], (C,), 1.0, 4.0, (), jnp.float32),
        "noise_gain": scatter_about(key_list[9], (C,), 1.5, 6.0, (), jnp.float32),
        "den_wb": scatter_about(key_list[10], (9, C, C), (9 * C) ** -0.5, 0.1875),
    }


SIGMA_DATA = 0.5
SIG_LOW = 0.25
SIG_HIGH = 4.0

def conv_taps(padded, weight, out_rows, out_cols):
    summed = jnp.zeros((weight.shape[1], out_rows, out_cols), jnp.float32)
    for tap_index in range(9):
        row_shift = tap_index // 3
        col_shift = tap_index % 3
        shifted = padded[:, row_shift:row_shift + out_rows, col_shift:col_shift + out_cols].astype(jnp.float32)
        summed = summed + jnp.einsum('oc,crw->orw', weight[tap_index].astype(jnp.float32), shifted)
    return summed

def pad_cells(field):
    return jnp.pad(field, ((0, 0), (1, 1), (1, 1)))

def reference(noisy, condition, levels, enc_w1, enc_b1, enc_w2, enc_b2, den_wa, den_ba, noise_gain, den_wb):
    enc_first = jax.nn.silu(conv_taps(pad_cells(condition), enc_w1, H, W) + enc_b1[:, None, None]).astype(jnp.bfloat16)
    enc_first = lax.optimization_barrier(enc_first)
    features = (conv_taps(pad_cells(enc_first), enc_w2, H, W) + enc_b2[:, None, None]).astype(jnp.bfloat16)
    features = lax.optimization_barrier(features)

    def one_member(packed):
        member_field, level_index = packed
        noise_sigma = SIG_LOW * (SIG_HIGH / SIG_LOW) ** (level_index.astype(jnp.float32) / (LEVELS - 1))
        spread = noise_sigma * noise_sigma + SIGMA_DATA * SIGMA_DATA
        c_in = 1.0 / jnp.sqrt(spread)
        c_skip = SIGMA_DATA * SIGMA_DATA / spread
        c_out = noise_sigma * SIGMA_DATA / jnp.sqrt(spread)
        c_noise = jnp.log(noise_sigma) / 4.0
        scaled = (c_in * member_field.astype(jnp.float32)).astype(jnp.bfloat16)
        joined = lax.optimization_barrier(jnp.concatenate([scaled, features], axis=0))
        before = conv_taps(pad_cells(joined), den_wa, H, W) + den_ba[:, None, None] + c_noise * noise_gain[:, None, None]
        hidden = lax.optimization_barrier(jax.nn.silu(before).astype(jnp.bfloat16))
        update = conv_taps(pad_cells(hidden), den_wb, H, W)
        return (c_skip * member_field.astype(jnp.float32) + c_out * update).astype(jnp.bfloat16)
    return lax.map(one_member, (noisy, levels))
```

```python
import functools

import jax
import jax.numpy as jnp
from jax import lax
from jax.experimental import pallas as pl
from jax.experimental.pallas import tpu as pltpu
from jax.sharding import PartitionSpec as P

LEVELS = 18
SIGMA_DATA = 0.5
SIG_LOW = 0.25
SIG_HIGH = 4.0

BF16 = jnp.bfloat16
F32 = jnp.float32
NT = (((1,), (1,)), ((), ()))
NN = (((1,), (0,)), ((), ()))
VMEM_LIMIT = 48 * 2**20

BASE = 8
HALO = 4
EDGE = 8
SLOT = 16


def prep_kernel(scale_ref, field_ref, pairs_ref, left_ref, right_ref, buf, *, pitch):
    chans, rows, cols = field_ref.shape
    buf[...] = field_ref[...].astype(F32).reshape(chans * rows, cols)
    c_in = scale_ref[0]
    for q in range(rows // 2):
        for h in range(2):
            row = buf[pl.ds(2 * q + h, chans, stride=rows), :]
            cells = (c_in * row.T).astype(BF16)
            lanes = slice(h * chans, (h + 1) * chans)
            pairs_ref[q * pitch + 2:q * pitch + 2 + cols, lanes] = cells
            left_ref[2 * q:2 * q + 2, lanes] = cells[:2]
            right_ref[2 * q:2 * q + 2, lanes] = cells[cols - 2:]


def pack_kernel(*refs, geo, block_count):
    top_ref, bottom_ref, left_ref, right_ref = refs[:4]
    blocks = refs[4:4 + block_count]
    outs = list(refs[4 + block_count:])
    n_strip, n_sub, n_member = geo["n_strip"], geo["n_sub"], geo["n_member"]
    pitch, cols, rows, cin = geo["pitch"], geo["cols"], geo["rows"], geo["cin"]
    half = cin // 2
    member = lax.axis_index("member")
    strip = lax.axis_index("strip")
    sub = lax.axis_index("sub")

    whole = outs[0]
    edge_rows = rows
    for k, block in enumerate(blocks):
        tall = block.shape[1]
        if block_count == 1:
            at = 0
        else:
            at = pl.multiple_of(lax.rem(member - k + n_member, n_member) * tall, tall)
        for c in range(cin):
            lanes = slice((c // half) * cols, (c // half + 1) * cols)
            start = 2 * (rows // 2) + (c % half) * rows + at
            if block_count != 1:
                start = pl.multiple_of(start, 16)
            whole[pl.ds(start, tall), lanes] = block[c]
    noisy_rows = 2 * (rows // 2)
    whole_left = left_ref[...]
    whole_right = right_ref[...]

    def cond_edge(c, top):
        lanes = slice((c // half) * cols, (c // half + 1) * cols)
        start = noisy_rows + (c % half) * rows
        if top:
            return whole[start:start + EDGE, lanes]
        return whole[start + rows - EDGE:start + rows, lanes]

    def pick(flag, a, b):
        return jnp.where(flag, a.astype(F32), b.astype(F32)).astype(BF16)

    def pair_edge(top):
        if top:
            return top_ref[2:2 + cols, :]
        return bottom_ref[pitch + 2:pitch + 2 + cols, :]

    if n_sub == 2:
        whole[:noisy_rows, :] = pick(sub == 0, whole_right, whole_left)
        rest = outs[1:]
    else:
        whole[:noisy_rows, :] = whole_left
        other = outs[1]
        other[noisy_rows:, :] = whole[noisy_rows:, :]
        other[:noisy_rows, :] = whole_right
        rest = outs[2:]
    tops = [None] if n_strip == 2 else [True, False]
    lefts = [None] if n_sub == 2 else [True, False]
    at = 0
    for top in tops:
        if top is None:
            pair = pick(strip == 0, pair_edge(False), pair_edge(True))
        else:
            pair = pair_edge(top)
        strip_out = rest[at]
        at += 1
        strip_out[:cols, :] = pair
        for c in range(cin):
            lanes = slice((c // half) * cols, (c // half + 1) * cols)
            if top is None:
                cells = pick(strip == 0, cond_edge(c, False), cond_edge(c, True))
            else:
                cells = cond_edge(c, top)
            start = cols + (c % half) * EDGE
            strip_out[start:start + EDGE, lanes] = cells
        for left in lefts:
            corner_out = rest[at]
            at += 1
            if left is None:
                corner = pick(sub == 0, pair[cols - 2:], pair[:2])
            else:
                corner = pair[:2] if left else pair[cols - 2:]
            corner_out[:2, :] = corner
            corner_out[16:, :] = strip_out[cols:, :]


def main_kernel(*refs, geo, n_strip_in, n_sub_in):
    it = iter(refs)
    scal = next(it)
    field_hbm = next(it)
    pairs_hbm = next(it)
    own = next(it)
    sub_in = [next(it) for _ in range(n_sub_in)]
    strip_in = []
    diag_in = []
    for _ in range(n_strip_in):
        strip_in.append(next(it))
        diag_in.append([next(it) for _ in range(n_sub_in)])
    w1, b1, w2, b2, wa, ba, gain, wb = [next(it) for _ in range(8)]
    out_hbm = next(it)
    (xe, xn, xf, xh, m1, m2, mn, mf, mb, cr, ch, lw, field, out, obuf, sems) = list(it)

    n_strip, n_sub = geo["n_strip"], geo["n_sub"]
    pitch, cols, rows, cin = geo["pitch"], geo["cols"], geo["rows"], geo["cin"]
    chans = 128
    half = cin // 2
    npair = rows // 2
    noisy_rows = 2 * npair
    strip = lax.axis_index("strip")
    sub = lax.axis_index("sub")
    above, below = strip > 0, strip < n_strip - 1
    before, after = sub > 0, sub < n_sub - 1

    get_pairs = pltpu.make_async_copy(
        pairs_hbm, xn.at[pl.ds(BASE + pitch, npair * pitch), :], sems.at[0])
    get_pairs.start()
    get_field = pltpu.make_async_copy(field_hbm, field, sems.at[1])
    get_field.start()

    def keep(flag, cells):
        return jnp.where(flag, cells.astype(F32), 0.0)

    def blocks_of(dst, src, lanes):
        zero = jnp.zeros((chans, chans), BF16)
        for b in range(3):
            a0 = b * 2 * chans
            b0 = (3 + b) * 2 * chans
            taps = [src[3 * a + b, :, lanes] for a in range(3)]
            dst[:chans, a0:a0 + chans] = taps[0]
            dst[:chans, a0 + chans:a0 + 2 * chans] = taps[1]
            dst[chans:, a0:a0 + chans] = zero
            dst[chans:, a0 + chans:a0 + 2 * chans] = taps[0]
            dst[:chans, b0:b0 + chans] = taps[2]
            dst[:chans, b0 + chans:b0 + 2 * chans] = zero
            dst[chans:, b0:b0 + chans] = taps[1]
            dst[chans:, b0 + chans:b0 + 2 * chans] = taps[2]

    blocks_of(m2, w2, slice(0, chans))
    blocks_of(mn, wa, slice(0, chans))
    blocks_of(mf, wa, slice(chans, 2 * chans))
    blocks_of(mb, wb, slice(0, chans))
    m1[...] = jnp.zeros_like(m1)
    for b in range(3):
        for n in range(6):
            for a in range(3):
                at = b * 8 * SLOT + (n + a) * SLOT
                m1[at:at + cin, n * chans:(n + 1) * chans] = w1[3 * a + b]

    cr[...] = jnp.zeros_like(cr)
    ch[...] = jnp.zeros_like(ch)

    def lanes_of(c):
        return slice((c // half) * cols, (c // half + 1) * cols)

    def fill(dst, body, tops):
        for c in range(cin):
            at = noisy_rows + (c % half) * rows
            dst[pl.ds(HALO * SLOT + c, rows, stride=SLOT), :] = (
                body[at:at + rows, lanes_of(c)].astype(F32))
            for source, flag, is_top, first in tops:
                at = first + (c % half) * EDGE
                cells = source[at:at + EDGE, lanes_of(c)].astype(F32)
                if is_top:
                    dst[pl.ds(c, HALO, stride=SLOT), :] = keep(flag, cells[EDGE - HALO:])
                else:
                    dst[pl.ds((HALO + rows) * SLOT + c, HALO, stride=SLOT), :] = keep(flag, cells[:HALO])

    strip_top, strip_bottom = strip_in[0], strip_in[-1]
    diag_top, diag_bottom = diag_in[0], diag_in[-1]
    fill(cr, own, [(strip_top, above, True, cols), (strip_bottom, below, False, cols)])
    windows = geo["windows"]
    for w in range(windows):
        cells = cr[6 * SLOT * w:6 * SLOT * w + 8 * SLOT, :].T
        at = BASE - HALO + w * pitch
        lw[at + HALO:at + HALO + cols, :] = cells.astype(BF16)
    for k in range(n_sub_in):
        fill(ch, sub_in[k], [(diag_top[k], above, True, 16), (diag_bottom[k], below, False, 16)])
        for w in range(windows):
            cells = ch[6 * SLOT * w:6 * SLOT * w + 8 * SLOT, :].T
            at = BASE - HALO + w * pitch
            if k == 0:
                lw[at:at + HALO, :] = keep(before, cells[cols - HALO:]).astype(BF16)
            if k == n_sub_in - 1:
                lw[at + HALO + cols:at + 2 * HALO + cols, :] = keep(after, cells[:HALO]).astype(BF16)

    def inside(y, left, right, first, count, low_row):
        y = y.reshape(count, pitch, 2 * chans)
        col = lax.broadcasted_iota(jnp.int32, (count, 8, 2 * chans), 1)
        head = jnp.where((col >= left) | before, y[:, :8], 0.0)
        tail = jnp.where((col < right - (pitch - 8)) | after, y[:, pitch - 8:], 0.0)
        y = jnp.concatenate([head, y[:, 8:pitch - 8], tail], axis=1)
        parts = []
        for i in range(count):
            halves = []
            for h in range(2):
                row = 2 * (first + i) + h - low_row
                cells = y[i, :, h * chans:(h + 1) * chans]
                if row < 0:
                    cells = jnp.where(above, cells, 0.0)
                elif row >= rows:
                    cells = jnp.where(below, cells, 0.0)
                halves.append(cells)
            parts.append(jnp.concatenate(halves, axis=1))
        return parts

    def silu(v):
        return v * (0.5 * jnp.tanh(0.5 * v) + 0.5)

    def twice(v):
        return jnp.concatenate([v, v], axis=1)

    bias1 = twice(b1[...])
    per = 4
    for w0 in range(0, windows, per):
        count = min(per, windows - w0)
        span = count * pitch
        at = BASE - HALO + w0 * pitch
        lhs = jnp.concatenate([lw[at + b:at + b + span, :] for b in range(3)], axis=1)
        y = lax.dot_general(lhs, m1[...], NN, preferred_element_type=F32)
        for p in range(3):
            z = silu(y[:, p * 2 * chans:(p + 1) * 2 * chans] + bias1)
            for i in range(count):
                j = 3 * (w0 + i) + p
                if j < npair + 3:
                    cells = inside(z[i * pitch:(i + 1) * pitch], 3, 3 + cols, j, 1, 3)[0]
                    xe[BASE + j * pitch:BASE + (j + 1) * pitch, :] = cells.astype(BF16)

    def conv(src, weight, first, count):
        span = count * pitch
        at = BASE + first * pitch
        lhs = jnp.concatenate(
            [src[at + p * pitch + b:at + p * pitch + b + span, :] for p in range(2) for b in range(3)],
            axis=1)
        return lax.dot_general(lhs, weight[...], NT, preferred_element_type=F32)

    def chunks(total, size):
        return [(at, min(size, total - at)) for at in range(0, total, size)]

    bias2 = twice(b2[...])
    for first, count in chunks(npair + 2, 9):
        parts = inside(conv(xe, m2, first, count) + bias2, 2, 2 + cols, first, count, 2)
        for i, cells in enumerate(parts):
            at = BASE + (first + i) * pitch
            xf[at:at + pitch, :] = cells.astype(BF16)

    get_pairs.wait()
    for k in range(n_sub_in):
        for q in range(npair):
            at = BASE + (q + 1) * pitch
            cells = sub_in[k][2 * q:2 * q + 2, :]
            if k == 0:
                xn[at:at + 2, :] = keep(before, cells).astype(BF16)
            if k == n_sub_in - 1:
                xn[at + 2 + cols:at + 4 + cols, :] = keep(after, cells).astype(BF16)
    for source, corners, flag, j in (
        (strip_top, diag_top, above, 0), (strip_bottom, diag_bottom, below, npair + 1)):
        at = BASE + j * pitch
        xn[at + 2:at + 2 + cols, :] = keep(flag, source[:cols, :]).astype(BF16)
        xn[at:at + 2, :] = keep(flag & before, corners[0][:2, :]).astype(BF16)
        xn[at + 2 + cols:at + 4 + cols, :] = keep(flag & after, corners[-1][:2, :]).astype(BF16)

    offset = twice(ba[...] + scal[3] * gain[...])
    for first, count in chunks(npair + 1, 9):
        y = conv(xn, mn, first, count) + conv(xf, mf, first, count) + offset
        parts = inside(silu(y), 1, 1 + cols, first, count, 1)
        for i, cells in enumerate(parts):
            at = BASE + (first + i) * pitch
            xh[at:at + pitch, :] = cells.astype(BF16)

    get_field.wait()
    c_skip, c_out = scal[1], scal[2]
    group = 8
    puts = []
    for first, count in chunks(npair, group):
        y = conv(xh, mb, first, count)
        tall = 2 * count
        for i in range(count):
            for h in range(2):
                cells = y[i * pitch:i * pitch + cols, h * chans:(h + 1) * chans]
                obuf[pl.ds(2 * i + h, chans, stride=tall), :] = cells.T
        update = obuf[...].reshape(chans, tall, cols)
        r0 = 2 * first
        skip = field[:, r0:r0 + tall, :].astype(F32)
        out[:, r0:r0 + tall, :] = (c_skip * skip + c_out * update).astype(BF16)
        put = pltpu.make_async_copy(
            out.at[:, pl.ds(r0, tall), :], out_hbm.at[:, pl.ds(r0, tall), :],
            sems.at[2 + first // group])
        put.start()
        puts.append(put)
    for put in puts:
        put.wait()


def local(
    noisy, condition, levels, enc_w1, enc_b1, enc_w2, enc_b2, den_wa, den_ba, noise_gain, den_wb
):
    field = noisy[0]
    chans, rows, cols = field.shape
    cin = condition.shape[0]
    n_member = lax.axis_size("member")
    n_strip = lax.axis_size("strip")
    n_sub = lax.axis_size("sub")
    pitch = cols + 2 * HALO
    npair = rows // 2
    geo = dict(n_strip=n_strip, n_sub=n_sub, n_member=n_member, pitch=pitch, cols=cols, rows=rows,
               cin=cin, windows=-(-(rows + 6) // 6))

    if n_member <= 4:
        blocks = [condition]
        for k in range(1, n_member):
            blocks.append(
                lax.ppermute(condition, "member", [(i, (i + k) % n_member) for i in range(n_member)]))
    else:
        blocks = [lax.all_gather(condition, "member", axis=1, tiled=True)]

    level_value = levels[0].astype(F32)
    noise_sigma = SIG_LOW * (SIG_HIGH / SIG_LOW) ** (level_value / (LEVELS - 1))
    spread = noise_sigma * noise_sigma + SIGMA_DATA * SIGMA_DATA
    c_in = 1.0 / jnp.sqrt(spread)
    c_skip = SIGMA_DATA * SIGMA_DATA / spread
    c_out = noise_sigma * SIGMA_DATA / jnp.sqrt(spread)
    c_noise = jnp.log(noise_sigma) / 4.0
    scal = jnp.stack([c_in, c_skip, c_out, c_noise])

    tall = 16
    steps = rows // tall
    pairs, left, right = pl.pallas_call(
        functools.partial(prep_kernel, pitch=pitch),
        grid=(steps,),
        out_shape=[
            jax.ShapeDtypeStruct((npair * pitch, 2 * chans), BF16),
            jax.ShapeDtypeStruct((2 * npair, 2 * chans), BF16),
            jax.ShapeDtypeStruct((2 * npair, 2 * chans), BF16),
        ],
        in_specs=[
            pl.BlockSpec(memory_space=pltpu.SMEM),
            pl.BlockSpec((chans, tall, cols), lambda i: (0, i, 0)),
        ],
        out_specs=[
            pl.BlockSpec((npair * pitch // steps, 2 * chans), lambda i: (i, 0)),
            pl.BlockSpec((2 * npair // steps, 2 * chans), lambda i: (i, 0)),
            pl.BlockSpec((2 * npair // steps, 2 * chans), lambda i: (i, 0)),
        ],
        scratch_shapes=[pltpu.VMEM((chans * tall, cols), F32)],
        compiler_params=pltpu.CompilerParams(vmem_limit_bytes=VMEM_LIMIT),
        cost_estimate=pl.CostEstimate(flops=0, bytes_accessed=16 * 2**20, transcendentals=0),
        name="prep",
    )(scal, field)

    whole_shape = jax.ShapeDtypeStruct((2 * npair + cin // 2 * rows, 2 * cols), BF16)
    strip_shape = jax.ShapeDtypeStruct((cols + cin // 2 * EDGE, 2 * cols), BF16)
    diag_shape = jax.ShapeDtypeStruct((16 + cin // 2 * EDGE, 2 * cols), BF16)
    n_sub_out = 1 if n_sub == 2 else 2
    n_strip_out = 1 if n_strip == 2 else 2
    out_shape = [whole_shape] * n_sub_out
    for _ in range(n_strip_out):
        out_shape += [strip_shape] + [diag_shape] * n_sub_out
    last = npair // 2 - 1
    vmem = pl.BlockSpec(memory_space=pltpu.VMEM)
    packed = pl.pallas_call(
        functools.partial(pack_kernel, geo=geo, block_count=len(blocks)),
        grid=(1,),
        out_shape=out_shape,
        in_specs=[
            pl.BlockSpec((2 * pitch, 2 * chans), lambda i: (0, 0)),
            pl.BlockSpec((2 * pitch, 2 * chans), lambda i: (last, 0)),
        ] + [vmem] * (2 + len(blocks)),
        out_specs=[vmem] * len(out_shape),
        compiler_params=pltpu.CompilerParams(vmem_limit_bytes=VMEM_LIMIT),
        name="pack",
    )(pairs, pairs, left, right, *blocks)

    def up(n):
        return [(i, i - 1) for i in range(1, n)]

    def down(n):
        return [(i, i + 1) for i in range(n - 1)]

    sub_moves = [up(n_sub) + down(n_sub)] if n_sub == 2 else [up(n_sub), down(n_sub)]
    strip_moves = [up(n_strip) + down(n_strip)] if n_strip == 2 else [up(n_strip), down(n_strip)]
    rest = packed[n_sub_out:]
    strip_in = []
    at = 0
    for move in strip_moves:
        got = [lax.ppermute(rest[at], "strip", move)]
        at += 1
        corners = []
        for side in sub_moves:
            pairs_of = [(i * n_sub + j, k * n_sub + l) for i, k in move for j, l in side]
            corners.append(lax.ppermute(rest[at], ("strip", "sub"), pairs_of))
            at += 1
        strip_in.append(got + corners[::-1])
    strip_in = [x for one in strip_in[::-1] for x in one]
    sub_in = [lax.ppermute(x, "sub", move) for x, move in zip(packed[:n_sub_out], sub_moves)][::-1]

    flat = BASE + (npair + 3) * pitch + 16
    windows = geo["windows"]
    any_spec = pl.BlockSpec(memory_space=pl.ANY)
    smem = pl.BlockSpec(memory_space=pltpu.SMEM)
    steps_out = -(-npair // 8)
    result = pl.pallas_call(
        functools.partial(main_kernel, geo=geo, n_strip_in=n_strip_out, n_sub_in=n_sub_out),
        out_shape=jax.ShapeDtypeStruct((chans, rows, cols), BF16),
        in_specs=[smem, any_spec, any_spec] + [vmem] * (1 + n_sub_out + len(strip_in) + 8),
        out_specs=any_spec,
        scratch_shapes=[
            pltpu.VMEM((flat, 2 * chans), BF16),
            pltpu.VMEM((flat, 2 * chans), BF16),
            pltpu.VMEM((flat, 2 * chans), BF16),
            pltpu.VMEM((flat, 2 * chans), BF16),
            pltpu.VMEM((3 * 8 * SLOT, 6 * chans), BF16),
            pltpu.VMEM((2 * chans, 12 * chans), BF16),
            pltpu.VMEM((2 * chans, 12 * chans), BF16),
            pltpu.VMEM((2 * chans, 12 * chans), BF16),
            pltpu.VMEM((2 * chans, 12 * chans), BF16),
            pltpu.VMEM(((6 * windows + 2) * SLOT, cols), F32),
            pltpu.VMEM(((6 * windows + 2) * SLOT, cols), F32),
            pltpu.VMEM((BASE + windows * pitch + 16, 8 * SLOT), BF16),
            pltpu.VMEM((chans, rows, cols), BF16),
            pltpu.VMEM((chans, rows, cols), BF16),
            pltpu.VMEM((chans * 16, cols), F32),
            pltpu.SemaphoreType.DMA((2 + steps_out,)),
        ],
        compiler_params=pltpu.CompilerParams(vmem_limit_bytes=VMEM_LIMIT),
        name="denoise",
    )(scal, field, pairs, packed[0], *sub_in, *strip_in, jnp.swapaxes(enc_w1, 1, 2),
      enc_b1[None], enc_w2, enc_b2[None], den_wa, den_ba[None], noise_gain[None], den_wb)
    return result[None]


def solution(mesh):
    return jax.shard_map(
        local,
        mesh=mesh,
        in_specs=(
            P(("group", "member"), None, "strip", "sub"),
            P("group", ("strip", "member"), "sub"),
            P(("group", "member")),
            P(),
            P(),
            P(),
            P(),
            P(),
            P(),
            P(),
            P(),
        ),
        out_specs=P(("group", "member"), None, "strip", "sub"),
        check_vma=False,
    )
```

```python
import functools
import math

import jax
import jax.numpy as jnp
from jax import lax
from jax.experimental import pallas as pl
from jax.experimental.pallas import tpu as pltpu
from jax.sharding import PartitionSpec as P

LEVELS = 18
SIGMA_DATA = 0.5
SIG_LOW = 0.25
SIG_HIGH = 4.0

BF16 = jnp.bfloat16
F32 = jnp.float32
NT = (((1,), (1,)), ((), ()))
NN = (((1,), (0,)), ((), ()))

BASE = 8
HALO = 4
EDGE = 8
GROUP = 8
SLOT = 16


def plan(level_ref):
    level = jnp.full((1, 128), level_ref[0].astype(F32))
    sigma = SIG_LOW * jnp.exp(level * (math.log(SIG_HIGH / SIG_LOW) / (LEVELS - 1)))
    spread = sigma * sigma + SIGMA_DATA * SIGMA_DATA
    root = jnp.sqrt(spread)
    return 1.0 / root, SIGMA_DATA * SIGMA_DATA / spread, sigma * SIGMA_DATA / root, jnp.log(sigma) / 4.0


def prep_kernel(level_ref, field_hbm, pairs_ref, left_ref, right_ref, raw, buf, sems, *, pitch):
    steps, chans, tall, cols = raw.shape
    gets = []
    for s in range(steps):
        get = pltpu.make_async_copy(field_hbm.at[:, pl.ds(s * tall, tall), :], raw.at[s], sems.at[s])
        get.start()
        gets.append(get)
    c_in = plan(level_ref)[0]
    for s in range(steps):
        gets[s].wait()
        buf[...] = raw[s].astype(F32).reshape(chans * tall, cols)
        for q in range(tall // 2):
            at = s * (tall // 2) + q
            for h in range(2):
                row = buf[pl.ds(2 * q + h, chans, stride=tall), :]
                cells = (c_in * row.T).astype(BF16)
                lanes = slice(h * chans, (h + 1) * chans)
                pairs_ref[at * pitch + 2:at * pitch + 2 + cols, lanes] = cells
                left_ref[2 * at:2 * at + 2, lanes] = cells[:2]
                right_ref[2 * at:2 * at + 2, lanes] = cells[cols - 2:]


def pack_kernel(*refs, geo, block_count):
    top_ref, bottom_ref, left_ref, right_ref = refs[:4]
    blocks = refs[4:4 + block_count]
    outs = list(refs[4 + block_count:])
    n_strip, n_sub, n_member = geo["n_strip"], geo["n_sub"], geo["n_member"]
    pitch, cols, rows, cin = geo["pitch"], geo["cols"], geo["rows"], geo["cin"]
    half = cin // 2
    member = lax.axis_index("member")
    strip = lax.axis_index("strip")
    sub = lax.axis_index("sub")

    whole = outs[0]
    edge_rows = rows
    for k, block in enumerate(blocks):
        tall = block.shape[1]
        if block_count == 1:
            at = 0
        else:
            at = pl.multiple_of(jnp.bitwise_xor(member, k) * tall, tall)
        for c in range(cin):
            lanes = slice((c // half) * cols, (c // half + 1) * cols)
            start = 2 * (rows // 2) + (c % half) * rows + at
            if block_count != 1:
                start = pl.multiple_of(start, 16)
            whole[pl.ds(start, tall), lanes] = block[c]
    noisy_rows = 2 * (rows // 2)
    whole_left = left_ref[...]
    whole_right = right_ref[...]

    def cond_edge(c, top):
        lanes = slice((c // half) * cols, (c // half + 1) * cols)
        start = noisy_rows + (c % half) * rows
        if top:
            return whole[start:start + EDGE, lanes]
        return whole[start + rows - EDGE:start + rows, lanes]

    def pick(flag, a, b):
        return jnp.where(flag, a.astype(F32), b.astype(F32)).astype(BF16)

    def pair_edge(top):
        if top:
            return top_ref[2:2 + cols, :]
        return bottom_ref[pitch + 2:pitch + 2 + cols, :]

    if n_sub == 2:
        whole[:noisy_rows, :] = pick(sub == 0, whole_right, whole_left)
        rest = outs[1:]
    else:
        whole[:noisy_rows, :] = whole_left
        other = outs[1]
        other[noisy_rows:, :] = whole[noisy_rows:, :]
        other[:noisy_rows, :] = whole_right
        rest = outs[2:]
    tops = [None] if n_strip == 2 else [True, False]
    lefts = [None] if n_sub == 2 else [True, False]
    at = 0
    for top in tops:
        if top is None:
            pair = pick(strip == 0, pair_edge(False), pair_edge(True))
        else:
            pair = pair_edge(top)
        strip_out = rest[at]
        at += 1
        strip_out[:cols, :] = pair
        for c in range(cin):
            lanes = slice((c // half) * cols, (c // half + 1) * cols)
            if top is None:
                cells = pick(strip == 0, cond_edge(c, False), cond_edge(c, True))
            else:
                cells = cond_edge(c, top)
            start = cols + (c % half) * EDGE
            strip_out[start:start + EDGE, lanes] = cells
        for left in lefts:
            corner_out = rest[at]
            at += 1
            if left is None:
                corner = pick(sub == 0, pair[cols - 2:], pair[:2])
            else:
                corner = pair[:2] if left else pair[cols - 2:]
            corner_out[:2, :] = corner
            corner_out[16:, :] = strip_out[cols:, :]


def conv(src, weight, at, span, pitch):
    lo, hi = slice(0, 128), slice(128, 256)
    parts = []
    for b in range(3):
        parts.append(src[at + b:at + b + span, hi])
        parts.append(src[at + pitch + b:at + pitch + b + span, lo])
    y = lax.dot_general(
        jnp.concatenate(parts, axis=1), weight[:, :768], NT, preferred_element_type=F32)
    more = span + 8
    upper = jnp.concatenate([src[at + b:at + b + more, lo] for b in range(2)], axis=1)
    upper = lax.dot_general(upper, weight[:, 768:1024], NT, preferred_element_type=F32)
    lower = jnp.concatenate(
        [src[at + pitch + b:at + pitch + b + more, hi] for b in range(2)], axis=1)
    lower = lax.dot_general(lower, weight[:, 1024:], NT, preferred_element_type=F32)
    return y + jnp.concatenate(
        [upper[:span, lo] + upper[1:span + 1, hi], lower[:span, lo] + lower[1:span + 1, hi]], axis=1)


def tiles_of(dst, src, lanes):
    zero = jnp.zeros((128, 128), BF16)
    tap = [[src[3 * a + b, :, lanes] for b in range(3)] for a in range(3)]

    def put(at, blocks):
        for n in range(2):
            for k in range(2):
                dst[n * 128:(n + 1) * 128, at + k * 128:at + (k + 1) * 128] = blocks[n][k]

    for b in range(3):
        put(b * 256, [[tap[1][b], tap[2][b]], [tap[0][b], tap[1][b]]])
    put(768, [[tap[0][0], tap[0][1]], [zero, tap[0][2]]])
    put(1024, [[tap[2][0], tap[2][1]], [zero, tap[2][2]]])


def chunks(total, size):
    return [(at, min(size, total - at)) for at in range(0, total, size)]


def noisy_kernel(pairs, w1, w2, wa, wb, part, m1, m2, mn, mf, mb, *, geo):
    pitch, npair, cin = geo["pitch"], geo["rows"] // 2, geo["cin"]
    chans = 128
    tiles_of(mn, wa, slice(0, chans))
    for first, count in chunks(npair - 1, GROUP):
        part[first * pitch:(first + count) * pitch, :] = conv(
            pairs, mn, first * pitch, count * pitch, pitch)
    tiles_of(m2, w2, slice(0, chans))
    tiles_of(mf, wa, slice(chans, 2 * chans))
    tiles_of(mb, wb, slice(0, chans))
    m1[...] = jnp.zeros_like(m1)
    for b in range(3):
        for n in range(6):
            for a in range(3):
                at = b * 8 * SLOT + (n + a) * SLOT
                m1[at:at + cin, n * chans:(n + 1) * chans] = w1[3 * a + b]


def main_kernel(*refs, geo, n_strip_in, n_sub_in):
    it = iter(refs)
    level_ref = next(it)
    field = next(it)
    part, pairs_top, pairs_bottom, left, right, own = [next(it) for _ in range(6)]
    sub_in = [next(it) for _ in range(n_sub_in)]
    strip_in = []
    diag_in = []
    for _ in range(n_strip_in):
        strip_in.append(next(it))
        diag_in.append([next(it) for _ in range(n_sub_in)])
    m1, m2, mn, mf, mb, b1, b2, ba, gain = [next(it) for _ in range(9)]
    out_hbm = next(it)
    (xe, xf, xh, xt, xb, xc, yc, cr, ch, lw, out, obuf, sems) = list(it)

    n_strip, n_sub = geo["n_strip"], geo["n_sub"]
    pitch, cols, rows, cin = geo["pitch"], geo["cols"], geo["rows"], geo["cin"]
    chans = 128
    half = cin // 2
    npair = rows // 2
    noisy_rows = 2 * npair
    strip = lax.axis_index("strip")
    sub = lax.axis_index("sub")
    above, below = strip > 0, strip < n_strip - 1
    before, after = sub > 0, sub < n_sub - 1

    _, c_skip, c_out, c_noise = plan(level_ref)

    def keep(flag, cells):
        return jnp.where(flag, cells.astype(F32), 0.0)

    cr[...] = jnp.zeros_like(cr)
    ch[...] = jnp.zeros_like(ch)

    def lanes_of(c):
        return slice((c // half) * cols, (c // half + 1) * cols)

    def fill(dst, body, tops):
        for c in range(cin):
            at = noisy_rows + (c % half) * rows
            dst[pl.ds(HALO * SLOT + c, rows, stride=SLOT), :] = (
                body[at:at + rows, lanes_of(c)].astype(F32))
            for source, flag, is_top, first in tops:
                at = first + (c % half) * EDGE
                cells = source[at:at + EDGE, lanes_of(c)].astype(F32)
                if is_top:
                    dst[pl.ds(c, HALO, stride=SLOT), :] = keep(flag, cells[EDGE - HALO:])
                else:
                    dst[pl.ds((HALO + rows) * SLOT + c, HALO, stride=SLOT), :] = keep(flag, cells[:HALO])

    strip_top, strip_bottom = strip_in[0], strip_in[-1]
    diag_top, diag_bottom = diag_in[0], diag_in[-1]
    fill(cr, own, [(strip_top, above, True, cols), (strip_bottom, below, False, cols)])
    windows = geo["windows"]
    for w in range(windows):
        cells = cr[6 * SLOT * w:6 * SLOT * w + 8 * SLOT, :].T
        at = BASE - HALO + w * pitch
        lw[at + HALO:at + HALO + cols, :] = cells.astype(BF16)
    for k in range(n_sub_in):
        fill(ch, sub_in[k], [(diag_top[k], above, True, 16), (diag_bottom[k], below, False, 16)])
        for w in range(windows):
            cells = ch[6 * SLOT * w:6 * SLOT * w + 8 * SLOT, :].T
            at = BASE - HALO + w * pitch
            if k == 0:
                lw[at:at + HALO, :] = keep(before, cells[cols - HALO:]).astype(BF16)
            if k == n_sub_in - 1:
                lw[at + HALO + cols:at + 2 * HALO + cols, :] = keep(after, cells[:HALO]).astype(BF16)

    def inside(y, left, right, first, count, low_row):
        y = y.reshape(count, pitch, 2 * chans)
        col = lax.broadcasted_iota(jnp.int32, (count, 8, 2 * chans), 1)
        head = jnp.where((col >= left) | before, y[:, :8], 0.0)
        tail = jnp.where((col < right - (pitch - 8)) | after, y[:, pitch - 8:], 0.0)
        y = jnp.concatenate([head, y[:, 8:pitch - 8], tail], axis=1)
        parts = []
        for i in range(count):
            halves = []
            for h in range(2):
                row = 2 * (first + i) + h - low_row
                cells = y[i, :, h * chans:(h + 1) * chans]
                if row < 0:
                    cells = jnp.where(above, cells, 0.0)
                elif row >= rows:
                    cells = jnp.where(below, cells, 0.0)
                halves.append(cells)
            parts.append(jnp.concatenate(halves, axis=1))
        return parts

    def silu(v):
        return v * (0.5 * jnp.tanh(0.5 * v) + 0.5)

    def twice(v):
        return jnp.concatenate([v, v], axis=1)

    bias1 = twice(b1[...])
    per = 4
    for w0 in range(0, windows, per):
        count = min(per, windows - w0)
        span = count * pitch
        at = BASE - HALO + w0 * pitch
        lhs = jnp.concatenate([lw[at + b:at + b + span, :] for b in range(3)], axis=1)
        y = lax.dot_general(lhs, m1[...], NN, preferred_element_type=F32)
        for p in range(3):
            z = silu(y[:, p * 2 * chans:(p + 1) * 2 * chans] + bias1)
            for i in range(count):
                j = 3 * (w0 + i) + p
                if j < npair + 3:
                    cells = inside(z[i * pitch:(i + 1) * pitch], 3, 3 + cols, j, 1, 3)[0]
                    xe[BASE + j * pitch:BASE + (j + 1) * pitch, :] = cells.astype(BF16)

    bias2 = twice(b2[...])
    for first, count in chunks(npair + 2, GROUP):
        y = conv(xe, m2, BASE + first * pitch, count * pitch, pitch) + bias2
        parts = inside(y, 2, 2 + cols, first, count, 2)
        for i, cells in enumerate(parts):
            at = BASE + (first + i) * pitch
            xf[at:at + pitch, :] = cells.astype(BF16)

    def halo_cells(q):
        return (keep(before, sub_in[0][2 * q:2 * q + 2, :]).astype(BF16),
                keep(after, sub_in[-1][2 * q:2 * q + 2, :]).astype(BF16))

    strip_rows = (
        (xt, strip_top, diag_top, above, 0, pairs_top[:pitch, :], 0, 1),
        (xb, strip_bottom, diag_bottom, below, 1, pairs_bottom[pitch:, :], npair - 1, 0))
    for dst, source, corners, flag, at, inner, q, inner_at in strip_rows:
        at = BASE + at * pitch
        dst[at + 2:at + 2 + cols, :] = keep(flag, source[:cols, :]).astype(BF16)
        dst[at:at + 2, :] = keep(flag & before, corners[0][:2, :]).astype(BF16)
        dst[at + 2 + cols:at + 4 + cols, :] = keep(flag & after, corners[-1][:2, :]).astype(BF16)
        at = BASE + inner_at * pitch
        dst[at:at + pitch, :] = inner
        dst[at:at + 2, :], dst[at + 2 + cols:at + 4 + cols, :] = halo_cells(q)
    for q in range(npair):
        at = 8 * q
        xc[at:at + 2, :], xc[at + 6:at + 8, :] = halo_cells(q)
        xc[at + 2:at + 4, :] = left[2 * q:2 * q + 2, :]
        xc[at + 4:at + 6, :] = right[2 * q:2 * q + 2, :]
    yc[...] = conv(xc, mn, 0, 8 * (npair - 1), 8)

    offset = twice(ba[...] + c_noise * gain[...])
    first_cols = lax.broadcasted_iota(jnp.int32, (8, 2 * chans), 0) < 2
    for first, count in chunks(npair + 1, GROUP):
        y = conv(xf, mf, BASE + first * pitch, count * pitch, pitch) + offset
        noisy = []
        for j in range(first, first + count):
            if j == 0:
                noisy.append(conv(xt, mn, BASE, pitch, pitch))
            elif j == npair:
                noisy.append(conv(xb, mn, BASE, pitch, pitch))
            else:
                at = (j - 1) * pitch
                edge = yc[8 * (j - 1):8 * j, :]
                noisy.append(jnp.where(first_cols, edge, part[at:at + 8, :]))
                noisy.append(part[at + 8:at + cols, :])
                noisy.append(jnp.where(
                    first_cols, pltpu.roll(edge, 4, 0), part[at + cols:at + cols + 8, :]))
        y = y + jnp.concatenate(noisy, axis=0)
        parts = inside(silu(y), 1, 1 + cols, first, count, 1)
        for i, cells in enumerate(parts):
            at = BASE + (first + i) * pitch
            xh[at:at + pitch, :] = cells.astype(BF16)

    c_skip, c_out = c_skip.reshape(1, 1, cols), c_out.reshape(1, 1, cols)
    puts = []
    for first, count in chunks(npair, 8):
        y = conv(xh, mb, BASE + first * pitch, count * pitch, pitch)
        tall = 2 * count
        for i in range(count):
            for h in range(2):
                cells = y[i * pitch:i * pitch + cols, h * chans:(h + 1) * chans]
                obuf[pl.ds(2 * i + h, chans, stride=tall), :] = cells.T
        update = obuf[...].reshape(chans, tall, cols)
        r0 = 2 * first
        skip = field[:, r0:r0 + tall, :].astype(F32)
        out[:, r0:r0 + tall, :] = (c_skip * skip + c_out * update).astype(BF16)
        put = pltpu.make_async_copy(
            out.at[:, pl.ds(r0, tall), :], out_hbm.at[:, pl.ds(r0, tall), :],
            sems.at[first // 8])
        put.start()
        puts.append(put)
    for put in puts:
        put.wait()


def local(
    noisy, condition, levels, enc_w1, enc_b1, enc_w2, enc_b2, den_wa, den_ba, noise_gain, den_wb
):
    field = noisy[0]
    chans, rows, cols = field.shape
    cin = condition.shape[0]
    n_member = lax.axis_size("member")
    n_strip = lax.axis_size("strip")
    n_sub = lax.axis_size("sub")
    pitch = cols + 2 * HALO
    npair = rows // 2
    geo = dict(n_strip=n_strip, n_sub=n_sub, n_member=n_member, pitch=pitch, cols=cols, rows=rows,
               cin=cin, windows=-(-(rows + 6) // 6))

    if n_member in (1, 2, 4):
        blocks = [condition]
        for k in range(1, n_member):
            blocks.append(
                lax.ppermute(condition, "member", [(i, i ^ k) for i in range(n_member)]))
    else:
        blocks = [lax.all_gather(condition, "member", axis=1, tiled=True)]

    tall = 16
    steps = rows // tall
    any_spec = pl.BlockSpec(memory_space=pl.ANY)
    smem = pl.BlockSpec(memory_space=pltpu.SMEM)
    vmem = pl.BlockSpec(memory_space=pltpu.VMEM)
    pairs, left, right = pl.pallas_call(
        functools.partial(prep_kernel, pitch=pitch),
        out_shape=[
            jax.ShapeDtypeStruct((npair * pitch + 16, 2 * chans), BF16),
            jax.ShapeDtypeStruct((2 * npair, 2 * chans), BF16),
            jax.ShapeDtypeStruct((2 * npair, 2 * chans), BF16),
        ],
        in_specs=[smem, pl.BlockSpec(memory_space=pltpu.HBM)],
        out_specs=[vmem] * 3,
        scratch_shapes=[
            pltpu.VMEM((steps, chans, tall, cols), BF16),
            pltpu.VMEM((chans * tall, cols), F32),
            pltpu.SemaphoreType.DMA((steps,)),
        ],
        compiler_params=pltpu.CompilerParams(vmem_limit_bytes=12 * 2**20),
        cost_estimate=pl.CostEstimate(flops=0, bytes_accessed=16 * 2**20, transcendentals=0),
        name="prep",
    )(levels, pltpu.with_memory_space_constraint(field, pltpu.HBM))

    whole_shape = jax.ShapeDtypeStruct((2 * npair + cin // 2 * rows, 2 * cols), BF16)
    strip_shape = jax.ShapeDtypeStruct((cols + cin // 2 * EDGE, 2 * cols), BF16)
    diag_shape = jax.ShapeDtypeStruct((16 + cin // 2 * EDGE, 2 * cols), BF16)
    n_sub_out = 1 if n_sub == 2 else 2
    n_strip_out = 1 if n_strip == 2 else 2
    out_shape = [whole_shape] * n_sub_out
    for _ in range(n_strip_out):
        out_shape += [strip_shape] + [diag_shape] * n_sub_out
    last = npair // 2 - 1
    packed = pl.pallas_call(
        functools.partial(pack_kernel, geo=geo, block_count=len(blocks)),
        grid=(1,),
        out_shape=out_shape,
        in_specs=[
            pl.BlockSpec((2 * pitch, 2 * chans), lambda i: (0, 0)),
            pl.BlockSpec((2 * pitch, 2 * chans), lambda i: (last, 0)),
        ] + [vmem] * (2 + len(blocks)),
        out_specs=[vmem] * len(out_shape),
        compiler_params=pltpu.CompilerParams(vmem_limit_bytes=8 * 2**20),
        name="pack",
    )(pairs, pairs, left, right, *blocks)

    def up(n):
        return [(i, i - 1) for i in range(1, n)]

    def down(n):
        return [(i, i + 1) for i in range(n - 1)]

    sub_moves = [up(n_sub) + down(n_sub)] if n_sub == 2 else [up(n_sub), down(n_sub)]
    strip_moves = [up(n_strip) + down(n_strip)] if n_strip == 2 else [up(n_strip), down(n_strip)]
    rest = packed[n_sub_out:]
    strip_in = []
    at = 0
    for move in strip_moves:
        got = [lax.ppermute(rest[at], "strip", move)]
        at += 1
        corners = []
        for side in sub_moves:
            pairs_of = [(i * n_sub + j, k * n_sub + l) for i, k in move for j, l in side]
            corners.append(lax.ppermute(rest[at], ("strip", "sub"), pairs_of))
            at += 1
        strip_in.append(got + corners[::-1])
    strip_in = [x for one in strip_in[::-1] for x in one]
    sub_in = [lax.ppermute(x, "sub", move) for x, move in zip(packed[:n_sub_out], sub_moves)][::-1]

    mat = jax.ShapeDtypeStruct((2 * chans, 10 * chans), BF16)
    part, *mats = pl.pallas_call(
        functools.partial(noisy_kernel, geo=geo),
        out_shape=[
            jax.ShapeDtypeStruct(((npair - 1) * pitch, 2 * chans), F32),
            jax.ShapeDtypeStruct((3 * 8 * SLOT, 6 * chans), BF16),
            mat, mat, mat, mat,
        ],
        in_specs=[vmem] * 5,
        out_specs=[vmem] * 6,
        compiler_params=pltpu.CompilerParams(vmem_limit_bytes=16 * 2**20),
        cost_estimate=pl.CostEstimate(
            flops=2 * 9 * chans * chans * rows * cols, bytes_accessed=8 * 2**20, transcendentals=0),
        name="noisy",
    )(pairs, jnp.swapaxes(enc_w1, 1, 2), enc_w2, den_wa, den_wb)

    flat = BASE + (npair + 3) * pitch + 16
    windows = geo["windows"]
    field_scratch = pltpu.VMEM((flat, 2 * chans), BF16)
    edge_scratch = pltpu.VMEM((BASE + 2 * pitch + 16, 2 * chans), BF16)
    cond_scratch = pltpu.VMEM(((6 * windows + 2) * SLOT, cols), F32)
    whole_scratch = pltpu.VMEM((chans, rows, cols), BF16)
    inputs = [part, pairs, pairs, left, right, packed[0], *sub_in, *strip_in, *mats,
              enc_b1[None], enc_b2[None], den_ba[None], noise_gain[None]]
    in_specs = [vmem] * len(inputs)
    in_specs[1] = pl.BlockSpec((2 * pitch, 2 * chans), lambda i: (0, 0))
    in_specs[2] = pl.BlockSpec((2 * pitch, 2 * chans), lambda i: (last, 0))
    result = pl.pallas_call(
        functools.partial(main_kernel, geo=geo, n_strip_in=n_strip_out, n_sub_in=n_sub_out),
        grid=(1,),
        out_shape=jax.ShapeDtypeStruct((chans, rows, cols), BF16),
        in_specs=[smem, vmem] + in_specs,
        out_specs=any_spec,
        scratch_shapes=[
            field_scratch, field_scratch, field_scratch,
            edge_scratch, edge_scratch,
            pltpu.VMEM((8 * npair + 16, 2 * chans), BF16),
            pltpu.VMEM((8 * (npair - 1), 2 * chans), F32),
            cond_scratch, cond_scratch,
            pltpu.VMEM((BASE + windows * pitch + 16, 8 * SLOT), BF16),
            whole_scratch,
            pltpu.VMEM((chans * 16, cols), F32),
            pltpu.SemaphoreType.DMA((-(-npair // 8),)),
        ],
        compiler_params=pltpu.CompilerParams(vmem_limit_bytes=28 * 2**20),
        name="denoise",
    )(levels, field, *inputs)
    return result[None]


def solution(mesh):
    return jax.shard_map(
        local,
        mesh=mesh,
        in_specs=(
            P(("group", "member"), None, "strip", "sub"),
            P("group", ("strip", "member"), "sub"),
            P(("group", "member")),
            P(),
            P(),
            P(),
            P(),
            P(),
            P(),
            P(),
            P(),
        ),
        out_specs=P(("group", "member"), None, "strip", "sub"),
        check_vma=False,
    )
```

```python
import functools
import math

import jax
import jax.numpy as jnp
from jax import lax
from jax.experimental import pallas as pl
from jax.experimental.pallas import tpu as pltpu
from jax.sharding import PartitionSpec as P

LEVELS = 18
SIGMA_DATA = 0.5
SIG_LOW = 0.25
SIG_HIGH = 4.0

BF16 = jnp.bfloat16
F32 = jnp.float32
NT = (((1,), (1,)), ((), ()))
NN = (((1,), (0,)), ((), ()))

BASE = 8
HALO = 4
EDGE = HALO
GROUP = 8
OUT_STRIDE = 17
SLOT = 16


def plan(level_ref):
    level = jnp.full((1, 128), level_ref[0].astype(F32))
    sigma = SIG_LOW * jnp.exp(level * (math.log(SIG_HIGH / SIG_LOW) / (LEVELS - 1)))
    spread = sigma * sigma + SIGMA_DATA * SIGMA_DATA
    root = jnp.sqrt(spread)
    return 1.0 / root, SIGMA_DATA * SIGMA_DATA / spread, sigma * SIGMA_DATA / root, jnp.log(sigma) / 4.0


def prep_kernel(level_ref, field_hbm, cond_hbm, pairs_ref, left_ref, right_ref, cond_ref, raw, buf,
                sems, *, pitch):
    steps, chans, tall, cols = raw.shape
    gets = []
    for s in range(steps):
        get = pltpu.make_async_copy(field_hbm.at[:, pl.ds(s * tall, tall), :], raw.at[s], sems.at[s])
        get.start()
        gets.append(get)
    get_cond = pltpu.make_async_copy(cond_hbm, cond_ref, sems.at[steps])
    get_cond.start()
    c_in = plan(level_ref)[0]
    for s in range(steps):
        gets[s].wait()
        buf[...] = raw[s].astype(F32).reshape(chans * tall, cols)
        for q in range(tall // 2):
            at = s * (tall // 2) + q
            for h in range(2):
                row = buf[pl.ds(2 * q + h, chans, stride=tall), :]
                cells = (c_in * row.T).astype(BF16)
                lanes = slice(h * chans, (h + 1) * chans)
                pairs_ref[at * pitch + 2:at * pitch + 2 + cols, lanes] = cells
                left_ref[2 * at:2 * at + 2, lanes] = cells[:2]
                right_ref[2 * at:2 * at + 2, lanes] = cells[cols - 2:]
    get_cond.wait()


def pack_kernel(*refs, geo, block_count):
    top_ref, bottom_ref, left_ref, right_ref = refs[:4]
    blocks = refs[4:4 + block_count]
    outs = list(refs[4 + block_count:])
    n_strip, n_sub, n_member = geo["n_strip"], geo["n_sub"], geo["n_member"]
    pitch, cols, rows, cin = geo["pitch"], geo["cols"], geo["rows"], geo["cin"]
    half = cin // 2
    member = lax.axis_index("member")
    strip = lax.axis_index("strip")
    sub = lax.axis_index("sub")

    whole = outs[0]
    edge_rows = rows
    for k, block in enumerate(blocks):
        tall = block.shape[1]
        if block_count == 1:
            at = 0
        else:
            at = pl.multiple_of(jnp.bitwise_xor(member, k) * tall, tall)
        for c in range(cin):
            lanes = slice((c // half) * cols, (c // half + 1) * cols)
            start = 2 * (rows // 2) + (c % half) * rows + at
            if block_count != 1:
                start = pl.multiple_of(start, 16)
            whole[pl.ds(start, tall), lanes] = block[c]
    noisy_rows = 2 * (rows // 2)
    whole_left = left_ref[...]
    whole_right = right_ref[...]

    def cond_edge(c, top):
        lanes = slice((c // half) * cols, (c // half + 1) * cols)
        start = noisy_rows + (c % half) * rows
        if top:
            return whole[start:start + EDGE, lanes]
        return whole[start + rows - EDGE:start + rows, lanes]

    def pick(flag, a, b):
        return jnp.where(flag, a.astype(F32), b.astype(F32)).astype(BF16)

    def pair_edge(top):
        if top:
            return top_ref[2:2 + cols, :]
        return bottom_ref[pitch + 2:pitch + 2 + cols, :]

    if n_sub == 2:
        whole[:noisy_rows, :] = pick(sub == 0, whole_right, whole_left)
        rest = outs[1:]
    else:
        whole[:noisy_rows, :] = whole_left
        other = outs[1]
        other[noisy_rows:, :] = whole[noisy_rows:, :]
        other[:noisy_rows, :] = whole_right
        rest = outs[2:]
    tops = [None] if n_strip == 2 else [True, False]
    lefts = [None] if n_sub == 2 else [True, False]
    at = 0
    for top in tops:
        if top is None:
            pair = pick(strip == 0, pair_edge(False), pair_edge(True))
        else:
            pair = pair_edge(top)
        strip_out = rest[at]
        at += 1
        strip_out[:cols, :] = pair
        for c in range(cin):
            lanes = slice((c // half) * cols, (c // half + 1) * cols)
            if top is None:
                cells = pick(strip == 0, cond_edge(c, False), cond_edge(c, True))
            else:
                cells = cond_edge(c, top)
            start = cols + (c % half) * EDGE
            strip_out[start:start + EDGE, lanes] = cells
        for left in lefts:
            corner_out = rest[at]
            at += 1
            if left is None:
                corner = pick(sub == 0, pair[cols - 2:], pair[:2])
            else:
                corner = pair[:2] if left else pair[cols - 2:]
            corner_out[:half * EDGE, :] = strip_out[cols:, :]
            corner_out[half * EDGE:half * EDGE + 2, :] = corner


def conv(pieces, weight):
    lo, hi = slice(0, 128), slice(128, 256)

    def rows_of(lanes, shift, extra):
        return jnp.concatenate(
            [src[at + shift(pitch):at + shift(pitch) + span + extra, lanes]
             for src, at, span, pitch in pieces], axis=0)

    inner = []
    for b in range(3):
        inner.append(rows_of(hi, lambda pitch: b, 0))
        inner.append(rows_of(lo, lambda pitch: pitch + b, 0))
    y = lax.dot_general(
        jnp.concatenate(inner, axis=1), weight[:, :768], NT, preferred_element_type=F32)
    upper = jnp.concatenate([rows_of(lo, lambda pitch: b, 8) for b in range(2)], axis=1)
    upper = lax.dot_general(upper, weight[:, 768:1024], NT, preferred_element_type=F32)
    lower = jnp.concatenate([rows_of(hi, lambda pitch: pitch + b, 8) for b in range(2)], axis=1)
    lower = lax.dot_general(lower, weight[:, 1024:], NT, preferred_element_type=F32)
    results = []
    at = more = 0
    for _, _, span, _ in pieces:
        a, b = upper[more:more + span + 8], lower[more:more + span + 8]
        outer = [a[:span, lo] + a[1:span + 1, hi], b[:span, lo] + b[1:span + 1, hi]]
        results.append(y[at:at + span] + jnp.concatenate(outer, axis=1))
        at += span
        more += span + 8
    return results


def tiles_of(dst, src, lanes):
    zero = jnp.zeros((128, 128), BF16)
    tap = [[src[3 * a + b, :, lanes] for b in range(3)] for a in range(3)]

    def put(at, blocks):
        for n in range(2):
            for k in range(2):
                dst[n * 128:(n + 1) * 128, at + k * 128:at + (k + 1) * 128] = blocks[n][k]

    for b in range(3):
        put(b * 256, [[tap[1][b], tap[2][b]], [tap[0][b], tap[1][b]]])
    put(768, [[tap[0][0], tap[0][1]], [zero, tap[0][2]]])
    put(1024, [[tap[2][0], tap[2][1]], [zero, tap[2][2]]])


def chunks(total, size):
    return [(at, min(size, total - at)) for at in range(0, total, size)]


def noisy_kernel(pairs, w1, w2, wa, wb, part, m1, m2, mn, mf, mb, *, geo):
    pitch, npair, cin = geo["pitch"], geo["rows"] // 2, geo["cin"]
    chans = 128
    tiles_of(mn, wa, slice(0, chans))
    for first, count in chunks(npair - 1, GROUP):
        part[first * pitch:(first + count) * pitch, :] = conv(
            [(pairs, first * pitch, count * pitch, pitch)], mn)[0]
    tiles_of(m2, w2, slice(0, chans))
    tiles_of(mf, wa, slice(chans, 2 * chans))
    tiles_of(mb, wb, slice(0, chans))
    m1[...] = jnp.zeros_like(m1)
    for b in range(3):
        for n in range(6):
            for a in range(3):
                at = b * 8 * SLOT + (n + a) * SLOT
                m1[at:at + cin, n * chans:(n + 1) * chans] = w1[3 * a + b]


def main_kernel(*refs, geo, n_strip_in, n_sub_in):
    it = iter(refs)
    level_ref = next(it)
    field = next(it)
    part, pairs_top, pairs_bottom, left, right, own = [next(it) for _ in range(6)]
    sub_in = [next(it) for _ in range(n_sub_in)]
    strip_in = []
    diag_in = []
    for _ in range(n_strip_in):
        strip_in.append(next(it))
        diag_in.append([next(it) for _ in range(n_sub_in)])
    m1, m2, mn, mf, mb, b1, b2, ba, gain = [next(it) for _ in range(9)]
    out_hbm = next(it)
    (xe, xf, xh, xt, xb, xc, yc, cr, ch, lw, out, obuf, sems) = list(it)

    n_strip, n_sub = geo["n_strip"], geo["n_sub"]
    pitch, cols, rows, cin = geo["pitch"], geo["cols"], geo["rows"], geo["cin"]
    chans = 128
    half = cin // 2
    npair = rows // 2
    noisy_rows = 2 * npair
    strip = lax.axis_index("strip")
    sub = lax.axis_index("sub")
    above, below = strip > 0, strip < n_strip - 1
    before, after = sub > 0, sub < n_sub - 1

    _, c_skip, c_out, c_noise = plan(level_ref)

    def keep(flag, cells):
        return jnp.where(flag, cells.astype(F32), 0.0)

    cr[...] = jnp.zeros_like(cr)
    ch[...] = jnp.zeros_like(ch)

    def lanes_of(c):
        return slice((c // half) * cols, (c // half + 1) * cols)

    def fill(dst, body, tops):
        for c in range(cin):
            at = noisy_rows + (c % half) * rows
            dst[pl.ds(HALO * SLOT + c, rows, stride=SLOT), :] = (
                body[at:at + rows, lanes_of(c)].astype(F32))
            for source, flag, is_top, first in tops:
                at = first + (c % half) * EDGE
                cells = source[at:at + EDGE, lanes_of(c)].astype(F32)
                if is_top:
                    dst[pl.ds(c, HALO, stride=SLOT), :] = keep(flag, cells[EDGE - HALO:])
                else:
                    dst[pl.ds((HALO + rows) * SLOT + c, HALO, stride=SLOT), :] = keep(flag, cells[:HALO])

    strip_top, strip_bottom = strip_in[0], strip_in[-1]
    diag_top, diag_bottom = diag_in[0], diag_in[-1]
    fill(cr, own, [(strip_top, above, True, cols), (strip_bottom, below, False, cols)])
    windows = geo["windows"]
    for w in range(windows):
        cells = cr[6 * SLOT * w:6 * SLOT * w + 8 * SLOT, :].T
        at = BASE - HALO + w * pitch
        lw[at + HALO:at + HALO + cols, :] = cells.astype(BF16)
    for k in range(n_sub_in):
        fill(ch, sub_in[k], [(diag_top[k], above, True, 0), (diag_bottom[k], below, False, 0)])
        for w in range(windows):
            cells = ch[6 * SLOT * w:6 * SLOT * w + 8 * SLOT, :].T
            at = BASE - HALO + w * pitch
            if k == 0:
                lw[at:at + HALO, :] = keep(before, cells[cols - HALO:]).astype(BF16)
            if k == n_sub_in - 1:
                lw[at + HALO + cols:at + 2 * HALO + cols, :] = keep(after, cells[:HALO]).astype(BF16)

    def inside(y, left, right, first, count, low_row):
        y = y.reshape(count, pitch, 2 * chans)
        col = lax.broadcasted_iota(jnp.int32, (count, 8, 2 * chans), 1)
        head = jnp.where((col >= left) | before, y[:, :8], 0.0)
        tail = jnp.where((col < right - (pitch - 8)) | after, y[:, pitch - 8:], 0.0)
        y = jnp.concatenate([head, y[:, 8:pitch - 8], tail], axis=1)
        parts = []
        for i in range(count):
            halves = []
            for h in range(2):
                row = 2 * (first + i) + h - low_row
                cells = y[i, :, h * chans:(h + 1) * chans]
                if row < 0:
                    cells = jnp.where(above, cells, 0.0)
                elif row >= rows:
                    cells = jnp.where(below, cells, 0.0)
                halves.append(cells)
            parts.append(jnp.concatenate(halves, axis=1))
        return parts

    def silu(v):
        return v * (0.5 * jnp.tanh(0.5 * v) + 0.5)

    def twice(v):
        return jnp.concatenate([v, v], axis=1)

    bias1 = twice(b1[...])
    per = 4
    for w0 in range(0, windows, per):
        count = min(per, windows - w0)
        span = count * pitch
        at = BASE - HALO + w0 * pitch
        lhs = jnp.concatenate([lw[at + b:at + b + span, :] for b in range(3)], axis=1)
        y = lax.dot_general(lhs, m1[...], NN, preferred_element_type=F32)
        for p in range(3):
            z = silu(y[:, p * 2 * chans:(p + 1) * 2 * chans] + bias1)
            for i in range(count):
                j = 3 * (w0 + i) + p
                if j < npair + 3:
                    cells = inside(z[i * pitch:(i + 1) * pitch], 3, 3 + cols, j, 1, 3)[0]
                    xe[BASE + j * pitch:BASE + (j + 1) * pitch, :] = cells.astype(BF16)

    bias2 = twice(b2[...])
    for first, count in chunks(npair + 2, GROUP):
        y = conv([(xe, BASE + first * pitch, count * pitch, pitch)], m2)[0] + bias2
        parts = inside(y, 2, 2 + cols, first, count, 2)
        for i, cells in enumerate(parts):
            at = BASE + (first + i) * pitch
            xf[at:at + pitch, :] = cells.astype(BF16)

    def halo_cells(q):
        return (keep(before, sub_in[0][2 * q:2 * q + 2, :]).astype(BF16),
                keep(after, sub_in[-1][2 * q:2 * q + 2, :]).astype(BF16))

    corner = slice(half * EDGE, half * EDGE + 2)
    strip_rows = (
        (xt, strip_top, diag_top, above, 0, pairs_top[:pitch, :], 0, 1),
        (xb, strip_bottom, diag_bottom, below, 1, pairs_bottom[pitch:, :], npair - 1, 0))
    for dst, source, corners, flag, at, inner, q, inner_at in strip_rows:
        at = BASE + at * pitch
        dst[at + 2:at + 2 + cols, :] = keep(flag, source[:cols, :]).astype(BF16)
        dst[at:at + 2, :] = keep(flag & before, corners[0][corner, :]).astype(BF16)
        dst[at + 2 + cols:at + 4 + cols, :] = keep(flag & after, corners[-1][corner, :]).astype(BF16)
        at = BASE + inner_at * pitch
        dst[at:at + pitch, :] = inner
        dst[at:at + 2, :], dst[at + 2 + cols:at + 4 + cols, :] = halo_cells(q)
    for q in range(npair):
        at = 8 * q
        xc[at:at + 2, :], xc[at + 6:at + 8, :] = halo_cells(q)
        xc[at + 2:at + 4, :] = left[2 * q:2 * q + 2, :]
        xc[at + 4:at + 6, :] = right[2 * q:2 * q + 2, :]
    edge_top, edge_bottom, edge_cols = conv(
        [(xt, BASE, pitch, pitch), (xb, BASE, pitch, pitch), (xc, 0, 8 * (npair - 1), 8)], mn)
    yc[...] = edge_cols

    offset = twice(ba[...] + c_noise * gain[...])
    first_cols = lax.broadcasted_iota(jnp.int32, (8, 2 * chans), 0) < 2
    for first, count in chunks(npair + 1, GROUP):
        y = conv([(xf, BASE + first * pitch, count * pitch, pitch)], mf)[0] + offset
        noisy = []
        for j in range(first, first + count):
            if j == 0:
                noisy.append(edge_top)
            elif j == npair:
                noisy.append(edge_bottom)
            else:
                at = (j - 1) * pitch
                edge = yc[8 * (j - 1):8 * j, :]
                noisy.append(jnp.where(first_cols, edge, part[at:at + 8, :]))
                noisy.append(part[at + 8:at + cols, :])
                noisy.append(jnp.where(
                    first_cols, pltpu.roll(edge, 4, 0), part[at + cols:at + cols + 8, :]))
        y = y + jnp.concatenate(noisy, axis=0)
        parts = inside(silu(y), 1, 1 + cols, first, count, 1)
        for i, cells in enumerate(parts):
            at = BASE + (first + i) * pitch
            xh[at:at + pitch, :] = cells.astype(BF16)

    puts = []
    for first, count in chunks(npair, 8):
        y = conv([(xh, BASE + first * pitch, count * pitch, pitch)], mb)[0]
        tall = 2 * count
        for i in range(count):
            for h in range(2):
                cells = y[i * pitch:i * pitch + cols, h * chans:(h + 1) * chans]
                obuf[pl.ds(2 * i + h, chans, stride=OUT_STRIDE), :] = cells.T
        r0 = 2 * first
        for c in range(chans):
            update = obuf[c * OUT_STRIDE:c * OUT_STRIDE + tall, :]
            skip = field[c, r0:r0 + tall, :].astype(F32)
            out[c, r0:r0 + tall, :] = (c_skip * skip + c_out * update).astype(BF16)
        put = pltpu.make_async_copy(
            out.at[:, pl.ds(r0, tall), :], out_hbm.at[:, pl.ds(r0, tall), :],
            sems.at[first // 8])
        put.start()
        puts.append(put)
    for put in puts:
        put.wait()


def local(
    noisy, condition, levels, enc_w1, enc_b1, enc_w2, enc_b2, den_wa, den_ba, noise_gain, den_wb
):
    field = noisy[0]
    chans, rows, cols = field.shape
    cin = condition.shape[0]
    n_member = lax.axis_size("member")
    n_strip = lax.axis_size("strip")
    n_sub = lax.axis_size("sub")
    pitch = cols + 2 * HALO
    npair = rows // 2
    geo = dict(n_strip=n_strip, n_sub=n_sub, n_member=n_member, pitch=pitch, cols=cols, rows=rows,
               cin=cin, windows=-(-(rows + 6) // 6))

    if n_member in (1, 2, 4):
        blocks = [condition]
        for k in range(1, n_member):
            blocks.append(
                lax.ppermute(condition, "member", [(i, i ^ k) for i in range(n_member)]))
    else:
        blocks = [lax.all_gather(condition, "member", axis=1, tiled=True)]

    tall = 16
    steps = rows // tall
    any_spec = pl.BlockSpec(memory_space=pl.ANY)
    smem = pl.BlockSpec(memory_space=pltpu.SMEM)
    vmem = pl.BlockSpec(memory_space=pltpu.VMEM)
    pairs, left, right, own_cond = pl.pallas_call(
        functools.partial(prep_kernel, pitch=pitch),
        out_shape=[
            jax.ShapeDtypeStruct((npair * pitch + 16, 2 * chans), BF16),
            jax.ShapeDtypeStruct((2 * npair, 2 * chans), BF16),
            jax.ShapeDtypeStruct((2 * npair, 2 * chans), BF16),
            jax.ShapeDtypeStruct(condition.shape, BF16),
        ],
        in_specs=[smem] + [pl.BlockSpec(memory_space=pltpu.HBM)] * 2,
        out_specs=[vmem] * 4,
        scratch_shapes=[
            pltpu.VMEM((steps, chans, tall, cols), BF16),
            pltpu.VMEM((chans * tall, cols), F32),
            pltpu.SemaphoreType.DMA((steps + 1,)),
        ],
        compiler_params=pltpu.CompilerParams(vmem_limit_bytes=12 * 2**20),
        cost_estimate=pl.CostEstimate(flops=0, bytes_accessed=16 * 2**20, transcendentals=0),
        name="prep",
    )(levels, pltpu.with_memory_space_constraint(field, pltpu.HBM),
      pltpu.with_memory_space_constraint(condition, pltpu.HBM))
    if len(blocks) > 1:
        blocks[0] = own_cond

    whole_shape = jax.ShapeDtypeStruct((2 * npair + cin // 2 * rows, 2 * cols), BF16)
    strip_shape = jax.ShapeDtypeStruct((cols + cin // 2 * EDGE, 2 * cols), BF16)
    diag_shape = jax.ShapeDtypeStruct((cin // 2 * EDGE + 8, 2 * cols), BF16)
    n_sub_out = 1 if n_sub == 2 else 2
    n_strip_out = 1 if n_strip == 2 else 2
    out_shape = [whole_shape] * n_sub_out
    for _ in range(n_strip_out):
        out_shape += [strip_shape] + [diag_shape] * n_sub_out
    last = npair // 2 - 1
    packed = pl.pallas_call(
        functools.partial(pack_kernel, geo=geo, block_count=len(blocks)),
        grid=(1,),
        out_shape=out_shape,
        in_specs=[
            pl.BlockSpec((2 * pitch, 2 * chans), lambda i: (0, 0)),
            pl.BlockSpec((2 * pitch, 2 * chans), lambda i: (last, 0)),
        ] + [vmem] * (2 + len(blocks)),
        out_specs=[vmem] * len(out_shape),
        compiler_params=pltpu.CompilerParams(vmem_limit_bytes=8 * 2**20),
        name="pack",
    )(pairs, pairs, left, right, *blocks)

    def up(n):
        return [(i, i - 1) for i in range(1, n)]

    def down(n):
        return [(i, i + 1) for i in range(n - 1)]

    sub_moves = [up(n_sub) + down(n_sub)] if n_sub == 2 else [up(n_sub), down(n_sub)]
    strip_moves = [up(n_strip) + down(n_strip)] if n_strip == 2 else [up(n_strip), down(n_strip)]
    rest = packed[n_sub_out:]
    strip_in = []
    at = 0
    for move in strip_moves:
        got = [lax.ppermute(rest[at], "strip", move)]
        at += 1
        corners = []
        for side in sub_moves:
            pairs_of = [(i * n_sub + j, k * n_sub + l) for i, k in move for j, l in side]
            corners.append(lax.ppermute(rest[at], ("strip", "sub"), pairs_of))
            at += 1
        strip_in.append(got + corners[::-1])
    strip_in = [x for one in strip_in[::-1] for x in one]
    sub_in = [lax.ppermute(x, "sub", move) for x, move in zip(packed[:n_sub_out], sub_moves)][::-1]

    mat = jax.ShapeDtypeStruct((2 * chans, 10 * chans), BF16)
    part, *mats = pl.pallas_call(
        functools.partial(noisy_kernel, geo=geo),
        out_shape=[
            jax.ShapeDtypeStruct(((npair - 1) * pitch, 2 * chans), F32),
            jax.ShapeDtypeStruct((3 * 8 * SLOT, 6 * chans), BF16),
            mat, mat, mat, mat,
        ],
        in_specs=[vmem] * 5,
        out_specs=[vmem] * 6,
        compiler_params=pltpu.CompilerParams(vmem_limit_bytes=16 * 2**20),
        cost_estimate=pl.CostEstimate(
            flops=2 * 9 * chans * chans * rows * cols, bytes_accessed=8 * 2**20, transcendentals=0),
        name="noisy",
    )(pairs, jnp.swapaxes(enc_w1, 1, 2), enc_w2, den_wa, den_wb)

    flat = BASE + (npair + 3) * pitch + 16
    windows = geo["windows"]
    field_scratch = pltpu.VMEM((flat, 2 * chans), BF16)
    edge_scratch = pltpu.VMEM((BASE + 2 * pitch + 16, 2 * chans), BF16)
    cond_scratch = pltpu.VMEM(((6 * windows + 2) * SLOT, cols), F32)
    whole_scratch = pltpu.VMEM((chans, rows, cols), BF16)
    inputs = [part, pairs, pairs, left, right, packed[0], *sub_in, *strip_in, *mats,
              enc_b1[None], enc_b2[None], den_ba[None], noise_gain[None]]
    in_specs = [vmem] * len(inputs)
    in_specs[1] = pl.BlockSpec((2 * pitch, 2 * chans), lambda i: (0, 0))
    in_specs[2] = pl.BlockSpec((2 * pitch, 2 * chans), lambda i: (last, 0))
    result = pl.pallas_call(
        functools.partial(main_kernel, geo=geo, n_strip_in=n_strip_out, n_sub_in=n_sub_out),
        grid=(1,),
        out_shape=jax.ShapeDtypeStruct((chans, rows, cols), BF16),
        in_specs=[smem, vmem] + in_specs,
        out_specs=any_spec,
        scratch_shapes=[
            field_scratch, field_scratch, field_scratch,
            edge_scratch, edge_scratch,
            pltpu.VMEM((8 * npair + 16, 2 * chans), BF16),
            pltpu.VMEM((8 * (npair - 1), 2 * chans), F32),
            cond_scratch, cond_scratch,
            pltpu.VMEM((BASE + windows * pitch + 16, 8 * SLOT), BF16),
            whole_scratch,
            pltpu.VMEM((chans * OUT_STRIDE, cols), F32),
            pltpu.SemaphoreType.DMA((-(-npair // 8),)),
        ],
        compiler_params=pltpu.CompilerParams(vmem_limit_bytes=28 * 2**20),
        name="denoise",
    )(levels, field, *inputs)
    return result[None]


def solution(mesh):
    return jax.shard_map(
        local,
        mesh=mesh,
        in_specs=(
            P(("group", "member"), None, "strip", "sub"),
            P("group", ("strip", "member"), "sub"),
            P(("group", "member")),
            P(),
            P(),
            P(),
            P(),
            P(),
            P(),
            P(),
            P(),
        ),
        out_specs=P(("group", "member"), None, "strip", "sub"),
        check_vma=False,
    )
```

```python
import functools
import math

import jax
import jax.numpy as jnp
from jax import lax
from jax.experimental import pallas as pl
from jax.experimental.pallas import tpu as pltpu
from jax.sharding import PartitionSpec as P

LEVELS = 18
SIGMA_DATA = 0.5
SIG_LOW = 0.25
SIG_HIGH = 4.0

BF16 = jnp.bfloat16
F32 = jnp.float32
NT = (((1,), (1,)), ((), ()))
NN = (((1,), (0,)), ((), ()))

BASE = 8
HALO = 4
EDGE = HALO
EARLY = 4
GROUP = 8
OUT_STRIDE = 17
HALO_ORDER = ("strip", "diag", "sub")
SLOT = 16


def plan(level_ref):
    level = level_ref[0:1, :]
    sigma = SIG_LOW * jnp.exp(level * (math.log(SIG_HIGH / SIG_LOW) / (LEVELS - 1)))
    spread = sigma * sigma + SIGMA_DATA * SIGMA_DATA
    root = jnp.sqrt(spread)
    return 1.0 / root, SIGMA_DATA * SIGMA_DATA / spread, sigma * SIGMA_DATA / root, jnp.log(sigma) / 4.0


def prep_kernel(level_ref, field_hbm, cond_hbm, pairs_ref, left_ref, right_ref, cond_ref, scale_ref,
                raw, buf, sems, *, pitch):
    steps, chans, tall, cols = raw.shape
    gets = []
    for s in range(steps):
        get = pltpu.make_async_copy(field_hbm.at[:, pl.ds(s * tall, tall), :], raw.at[s], sems.at[s])
        get.start()
        gets.append(get)
    get_cond = pltpu.make_async_copy(cond_hbm, cond_ref, sems.at[steps])
    get_cond.start()
    c_in, c_skip, c_out, c_noise = plan(level_ref)
    scale_ref[...] = jnp.concatenate(
        [c_skip, c_out, c_noise, jnp.zeros((5, 128), F32)], axis=0)
    for s in range(steps):
        gets[s].wait()
        buf[...] = raw[s].astype(F32).reshape(chans * tall, cols)
        for q in range(tall // 2):
            at = s * (tall // 2) + q
            for h in range(2):
                row = buf[pl.ds(2 * q + h, chans, stride=tall), :]
                cells = (c_in * row.T).astype(BF16)
                lanes = slice(h * chans, (h + 1) * chans)
                pairs_ref[at * pitch + 2:at * pitch + 2 + cols, lanes] = cells
                left_ref[2 * at:2 * at + 2, lanes] = cells[:2]
                right_ref[2 * at:2 * at + 2, lanes] = cells[cols - 2:]
    get_cond.wait()


def pack_kernel(*refs, geo, order):
    block_count = len(order)
    top_ref, bottom_ref, left_ref, right_ref = refs[:4]
    blocks = [refs[4 + order.index(k)] for k in range(block_count)]
    outs = list(refs[4 + block_count + 1:])
    n_strip, n_sub, n_member = geo["n_strip"], geo["n_sub"], geo["n_member"]
    pitch, cols, rows, cin = geo["pitch"], geo["cols"], geo["rows"], geo["cin"]
    half = cin // 2
    member = lax.axis_index("member")
    strip = lax.axis_index("strip")
    sub = lax.axis_index("sub")

    n_sub_out = 1 if n_sub == 2 else 2
    rest, subs = outs[:-n_sub_out], outs[-n_sub_out:]
    whole = subs[0]
    for k, block in enumerate(blocks):
        tall = block.shape[1]
        if block_count == 1:
            at = 0
        else:
            at = pl.multiple_of(jnp.bitwise_xor(member, k) * tall, tall)
        for c in range(cin):
            lanes = slice((c // half) * cols, (c // half + 1) * cols)
            start = 2 * (rows // 2) + (c % half) * rows + at
            if block_count != 1:
                start = pl.multiple_of(start, 16)
            whole[pl.ds(start, tall), lanes] = block[c]
    noisy_rows = 2 * (rows // 2)
    whole_left = left_ref[...]
    whole_right = right_ref[...]

    def cond_edge(c, top):
        lanes = slice((c // half) * cols, (c // half + 1) * cols)
        start = noisy_rows + (c % half) * rows
        if top:
            return whole[start:start + EDGE, lanes]
        return whole[start + rows - EDGE:start + rows, lanes]

    def pick(flag, a, b):
        return jnp.where(flag, a.astype(F32), b.astype(F32)).astype(BF16)

    def pair_edge(top):
        if top:
            return top_ref[2:2 + cols, :]
        return bottom_ref[pitch + 2:pitch + 2 + cols, :]

    if n_sub == 2:
        whole[:noisy_rows, :] = pick(sub == 0, whole_right, whole_left)
    else:
        whole[:noisy_rows, :] = whole_left
        other = subs[1]
        other[noisy_rows:, :] = whole[noisy_rows:, :]
        other[:noisy_rows, :] = whole_right
    tops = [None] if n_strip == 2 else [True, False]
    lefts = [None] if n_sub == 2 else [True, False]
    at = 0
    for top in tops:
        if top is None:
            pair = pick(strip == 0, pair_edge(False), pair_edge(True))
        else:
            pair = pair_edge(top)
        strip_out = rest[at]
        at += 1
        strip_out[:cols, :] = pair
        for c in range(cin):
            lanes = slice((c // half) * cols, (c // half + 1) * cols)
            if top is None:
                cells = pick(strip == 0, cond_edge(c, False), cond_edge(c, True))
            else:
                cells = cond_edge(c, top)
            start = cols + (c % half) * EDGE
            strip_out[start:start + EDGE, lanes] = cells
        for left in lefts:
            corner_out = rest[at]
            at += 1
            if left is None:
                corner = pick(sub == 0, pair[cols - 2:], pair[:2])
            else:
                corner = pair[:2] if left else pair[cols - 2:]
            corner_out[:half * EDGE, :] = strip_out[cols:, :]
            corner_out[half * EDGE:half * EDGE + 2, :] = corner


def conv(pieces, weight):
    lo, hi = slice(0, 128), slice(128, 256)

    def rows_of(lanes, shift, extra):
        return jnp.concatenate(
            [src[at + shift(pitch):at + shift(pitch) + span + extra, lanes]
             for src, at, span, pitch in pieces], axis=0)

    inner = []
    for b in range(3):
        inner.append(rows_of(hi, lambda pitch: b, 0))
        inner.append(rows_of(lo, lambda pitch: pitch + b, 0))
    y = lax.dot_general(
        jnp.concatenate(inner, axis=1), weight[:, :768], NT, preferred_element_type=F32)
    upper = jnp.concatenate([rows_of(lo, lambda pitch: b, 8) for b in range(2)], axis=1)
    upper = lax.dot_general(upper, weight[:, 768:1024], NT, preferred_element_type=F32)
    lower = jnp.concatenate([rows_of(hi, lambda pitch: pitch + b, 8) for b in range(2)], axis=1)
    lower = lax.dot_general(lower, weight[:, 1024:], NT, preferred_element_type=F32)
    results = []
    at = more = 0
    for _, _, span, _ in pieces:
        a, b = upper[more:more + span + 8], lower[more:more + span + 8]
        outer = [a[:span, lo] + a[1:span + 1, hi], b[:span, lo] + b[1:span + 1, hi]]
        results.append(y[at:at + span] + jnp.concatenate(outer, axis=1))
        at += span
        more += span + 8
    return results


def tiles_of(dst, src, lanes):
    zero = jnp.zeros((128, 128), BF16)
    tap = [[src[3 * a + b, :, lanes] for b in range(3)] for a in range(3)]

    def put(at, blocks):
        for n in range(2):
            for k in range(2):
                dst[n * 128:(n + 1) * 128, at + k * 128:at + (k + 1) * 128] = blocks[n][k]

    for b in range(3):
        put(b * 256, [[tap[1][b], tap[2][b]], [tap[0][b], tap[1][b]]])
    put(768, [[tap[0][0], tap[0][1]], [zero, tap[0][2]]])
    put(1024, [[tap[2][0], tap[2][1]], [zero, tap[2][2]]])


def chunks(total, size):
    return [(at, min(size, total - at)) for at in range(0, total, size)]


def first_kernel(pairs, wa, part, mn, *, pitch):
    tiles_of(mn, wa, slice(0, 128))
    for first, count in chunks(part.shape[0] // pitch, GROUP):
        part[first * pitch:(first + count) * pitch, :] = conv(
            [(pairs, first * pitch, count * pitch, pitch)], mn)[0]


def second_kernel(pairs, mn, w1, w2, wa, wb, part, m1, m2, mf, mb, *, geo, skip):
    pitch, cin = geo["pitch"], geo["cin"]
    chans = 128
    for first, count in chunks(part.shape[0] // pitch, GROUP):
        part[first * pitch:(first + count) * pitch, :] = conv(
            [(pairs, (skip + first) * pitch, count * pitch, pitch)], mn)[0]
    tiles_of(m2, w2, slice(0, chans))
    tiles_of(mf, wa, slice(chans, 2 * chans))
    tiles_of(mb, wb, slice(0, chans))
    m1[...] = jnp.zeros_like(m1)
    for b in range(3):
        for n in range(6):
            for a in range(3):
                at = b * 8 * SLOT + (n + a) * SLOT
                m1[at:at + cin, n * chans:(n + 1) * chans] = w1[3 * a + b]


def main_kernel(*refs, geo, n_strip_in, n_sub_in):
    it = iter(refs)
    scales = next(it)
    field = next(it)
    part_a, part_b, pairs_top, pairs_bottom, left, right, own = [next(it) for _ in range(7)]
    split = part_a.shape[0] // geo["pitch"]
    got = {}
    for kind in HALO_ORDER:
        count = dict(strip=n_strip_in, sub=n_sub_in, diag=n_strip_in * n_sub_in)[kind]
        got[kind] = [next(it) for _ in range(count)]
    strip_in, sub_in = got["strip"], got["sub"]
    diag_in = [got["diag"][k * n_sub_in:(k + 1) * n_sub_in] for k in range(n_strip_in)]
    m1, m2, mn, mf, mb, b1, b2, ba, gain = [next(it) for _ in range(9)]
    out_hbm = next(it)
    (xe, xf, xh, xt, xb, xc, yc, cr, ch, lw, out, obuf, sems) = list(it)

    n_strip, n_sub = geo["n_strip"], geo["n_sub"]
    pitch, cols, rows, cin = geo["pitch"], geo["cols"], geo["rows"], geo["cin"]
    chans = 128
    half = cin // 2
    npair = rows // 2
    noisy_rows = 2 * npair
    strip = lax.axis_index("strip")
    sub = lax.axis_index("sub")
    above, below = strip > 0, strip < n_strip - 1
    before, after = sub > 0, sub < n_sub - 1

    c_skip, c_out, c_noise = scales[0:1, :], scales[1:2, :], scales[2:3, :]

    def keep(flag, cells):
        return jnp.where(flag, cells.astype(F32), 0.0)

    cr[...] = jnp.zeros_like(cr)
    ch[...] = jnp.zeros_like(ch)

    def lanes_of(c):
        return slice((c // half) * cols, (c // half + 1) * cols)

    def fill(dst, body, tops):
        for c in range(cin):
            at = noisy_rows + (c % half) * rows
            dst[pl.ds(HALO * SLOT + c, rows, stride=SLOT), :] = (
                body[at:at + rows, lanes_of(c)].astype(F32))
            for source, flag, is_top, first in tops:
                at = first + (c % half) * EDGE
                cells = source[at:at + EDGE, lanes_of(c)].astype(F32)
                if is_top:
                    dst[pl.ds(c, HALO, stride=SLOT), :] = keep(flag, cells[EDGE - HALO:])
                else:
                    dst[pl.ds((HALO + rows) * SLOT + c, HALO, stride=SLOT), :] = keep(flag, cells[:HALO])

    strip_top, strip_bottom = strip_in[0], strip_in[-1]
    diag_top, diag_bottom = diag_in[0], diag_in[-1]
    fill(cr, own, [(strip_top, above, True, cols), (strip_bottom, below, False, cols)])
    windows = geo["windows"]
    for w in range(windows):
        cells = cr[6 * SLOT * w:6 * SLOT * w + 8 * SLOT, :].T
        at = BASE - HALO + w * pitch
        lw[at + HALO:at + HALO + cols, :] = cells.astype(BF16)
    for k in range(n_sub_in):
        fill(ch, sub_in[k], [(diag_top[k], above, True, 0), (diag_bottom[k], below, False, 0)])
        for w in range(windows):
            cells = ch[6 * SLOT * w:6 * SLOT * w + 8 * SLOT, :].T
            at = BASE - HALO + w * pitch
            if k == 0:
                lw[at:at + HALO, :] = keep(before, cells[cols - HALO:]).astype(BF16)
            if k == n_sub_in - 1:
                lw[at + HALO + cols:at + 2 * HALO + cols, :] = keep(after, cells[:HALO]).astype(BF16)

    def inside(y, left, right, first, count, low_row):
        y = y.reshape(count, pitch, 2 * chans)
        col = lax.broadcasted_iota(jnp.int32, (count, 8, 2 * chans), 1)
        head = jnp.where((col >= left) | before, y[:, :8], 0.0)
        tail = jnp.where((col < right - (pitch - 8)) | after, y[:, pitch - 8:], 0.0)
        y = jnp.concatenate([head, y[:, 8:pitch - 8], tail], axis=1)
        parts = []
        for i in range(count):
            halves = []
            for h in range(2):
                row = 2 * (first + i) + h - low_row
                cells = y[i, :, h * chans:(h + 1) * chans]
                if row < 0:
                    cells = jnp.where(above, cells, 0.0)
                elif row >= rows:
                    cells = jnp.where(below, cells, 0.0)
                halves.append(cells)
            parts.append(jnp.concatenate(halves, axis=1))
        return parts

    def silu(v):
        return v * (0.5 * jnp.tanh(0.5 * v) + 0.5)

    def twice(v):
        return jnp.concatenate([v, v], axis=1)

    bias1 = twice(b1[...])
    per = 4
    for w0 in range(0, windows, per):
        count = min(per, windows - w0)
        span = count * pitch
        at = BASE - HALO + w0 * pitch
        lhs = jnp.concatenate([lw[at + b:at + b + span, :] for b in range(3)], axis=1)
        y = lax.dot_general(lhs, m1[...], NN, preferred_element_type=F32)
        for p in range(3):
            z = silu(y[:, p * 2 * chans:(p + 1) * 2 * chans] + bias1)
            for i in range(count):
                j = 3 * (w0 + i) + p
                if j < npair + 3:
                    cells = inside(z[i * pitch:(i + 1) * pitch], 3, 3 + cols, j, 1, 3)[0]
                    xe[BASE + j * pitch:BASE + (j + 1) * pitch, :] = cells.astype(BF16)

    bias2 = twice(b2[...])
    for first, count in chunks(npair + 2, GROUP):
        y = conv([(xe, BASE + first * pitch, count * pitch, pitch)], m2)[0] + bias2
        parts = inside(y, 2, 2 + cols, first, count, 2)
        for i, cells in enumerate(parts):
            at = BASE + (first + i) * pitch
            xf[at:at + pitch, :] = cells.astype(BF16)

    def halo_cells(q):
        return (keep(before, sub_in[0][2 * q:2 * q + 2, :]).astype(BF16),
                keep(after, sub_in[-1][2 * q:2 * q + 2, :]).astype(BF16))

    corner = slice(half * EDGE, half * EDGE + 2)
    strip_rows = (
        (xt, strip_top, diag_top, above, 0, pairs_top[:pitch, :], 0, 1),
        (xb, strip_bottom, diag_bottom, below, 1, pairs_bottom[pitch:, :], npair - 1, 0))
    for dst, source, corners, flag, at, inner, q, inner_at in strip_rows:
        at = BASE + at * pitch
        dst[at + 2:at + 2 + cols, :] = keep(flag, source[:cols, :]).astype(BF16)
        dst[at:at + 2, :] = keep(flag & before, corners[0][corner, :]).astype(BF16)
        dst[at + 2 + cols:at + 4 + cols, :] = keep(flag & after, corners[-1][corner, :]).astype(BF16)
        at = BASE + inner_at * pitch
        dst[at:at + pitch, :] = inner
        dst[at:at + 2, :], dst[at + 2 + cols:at + 4 + cols, :] = halo_cells(q)
    for q in range(npair):
        at = 8 * q
        xc[at:at + 2, :], xc[at + 6:at + 8, :] = halo_cells(q)
        xc[at + 2:at + 4, :] = left[2 * q:2 * q + 2, :]
        xc[at + 4:at + 6, :] = right[2 * q:2 * q + 2, :]
    edge_top, edge_bottom, edge_cols = conv(
        [(xt, BASE, pitch, pitch), (xb, BASE, pitch, pitch), (xc, 0, 8 * (npair - 1), 8)], mn)
    yc[...] = edge_cols

    offset = twice(ba[...] + c_noise * gain[...])
    first_cols = lax.broadcasted_iota(jnp.int32, (8, 2 * chans), 0) < 2
    for first, count in chunks(npair + 1, GROUP):
        y = conv([(xf, BASE + first * pitch, count * pitch, pitch)], mf)[0] + offset
        noisy = []
        for j in range(first, first + count):
            if j == 0:
                noisy.append(edge_top)
            elif j == npair:
                noisy.append(edge_bottom)
            else:
                part, at = (part_a, j - 1) if j - 1 < split else (part_b, j - 1 - split)
                at *= pitch
                edge = yc[8 * (j - 1):8 * j, :]
                noisy.append(jnp.where(first_cols, edge, part[at:at + 8, :]))
                noisy.append(part[at + 8:at + cols, :])
                noisy.append(jnp.where(
                    first_cols, pltpu.roll(edge, 4, 0), part[at + cols:at + cols + 8, :]))
        y = y + jnp.concatenate(noisy, axis=0)
        parts = inside(silu(y), 1, 1 + cols, first, count, 1)
        for i, cells in enumerate(parts):
            at = BASE + (first + i) * pitch
            xh[at:at + pitch, :] = cells.astype(BF16)

    puts = []
    for first, count in chunks(npair, 8):
        y = conv([(xh, BASE + first * pitch, count * pitch, pitch)], mb)[0]
        tall = 2 * count
        for i in range(count):
            for h in range(2):
                cells = y[i * pitch:i * pitch + cols, h * chans:(h + 1) * chans]
                obuf[pl.ds(2 * i + h, chans, stride=OUT_STRIDE), :] = cells.T
        r0 = 2 * first
        for c in range(chans):
            update = obuf[c * OUT_STRIDE:c * OUT_STRIDE + tall, :]
            skip = field[c, r0:r0 + tall, :].astype(F32)
            out[c, r0:r0 + tall, :] = (c_skip * skip + c_out * update).astype(BF16)
        put = pltpu.make_async_copy(
            out.at[:, pl.ds(r0, tall), :], out_hbm.at[:, pl.ds(r0, tall), :],
            sems.at[first // 8])
        put.start()
        puts.append(put)
    for put in puts:
        put.wait()


def local(
    noisy, condition, levels, enc_w1, enc_b1, enc_w2, enc_b2, den_wa, den_ba, noise_gain, den_wb
):
    field = noisy[0]
    chans, rows, cols = field.shape
    cin = condition.shape[0]
    n_member = lax.axis_size("member")
    n_strip = lax.axis_size("strip")
    n_sub = lax.axis_size("sub")
    pitch = cols + 2 * HALO
    npair = rows // 2
    geo = dict(n_strip=n_strip, n_sub=n_sub, n_member=n_member, pitch=pitch, cols=cols, rows=rows,
               cin=cin, windows=-(-(rows + 6) // 6))

    if n_member in (1, 2, 4):
        blocks = [condition]
        for k in range(1, n_member):
            blocks.append(
                lax.ppermute(condition, "member", [(i, i ^ k) for i in range(n_member)]))
    else:
        blocks = [lax.all_gather(condition, "member", axis=1, tiled=True)]

    tall = 16
    steps = rows // tall
    any_spec = pl.BlockSpec(memory_space=pl.ANY)
    vmem = pl.BlockSpec(memory_space=pltpu.VMEM)
    pairs, left, right, own_cond, scales = pl.pallas_call(
        functools.partial(prep_kernel, pitch=pitch),
        out_shape=[
            jax.ShapeDtypeStruct((npair * pitch + 16, 2 * chans), BF16),
            jax.ShapeDtypeStruct((2 * npair, 2 * chans), BF16),
            jax.ShapeDtypeStruct((2 * npair, 2 * chans), BF16),
            jax.ShapeDtypeStruct(condition.shape, BF16),
            jax.ShapeDtypeStruct((8, 128), F32),
        ],
        in_specs=[vmem] + [pl.BlockSpec(memory_space=pltpu.HBM)] * 2,
        out_specs=[vmem] * 5,
        scratch_shapes=[
            pltpu.VMEM((steps, chans, tall, cols), BF16),
            pltpu.VMEM((chans * tall, cols), F32),
            pltpu.SemaphoreType.DMA((steps + 1,)),
        ],
        compiler_params=pltpu.CompilerParams(vmem_limit_bytes=12 * 2**20),
        cost_estimate=pl.CostEstimate(flops=0, bytes_accessed=16 * 2**20, transcendentals=0),
        name="prep",
    )(jnp.broadcast_to(levels.astype(F32)[:, None], (8, 128)), *[pltpu.with_memory_space_constraint(x, pltpu.HBM) for x in (field, condition)])
    if len(blocks) > 1:
        blocks[0] = own_cond

    mat = jax.ShapeDtypeStruct((2 * chans, 10 * chans), BF16)
    work = 2 * 9 * chans * chans * 2 * cols
    split = EARLY
    part_a, mn = pl.pallas_call(
        functools.partial(first_kernel, pitch=pitch),
        out_shape=[jax.ShapeDtypeStruct((split * pitch, 2 * chans), F32), mat],
        in_specs=[vmem] * 2,
        out_specs=[vmem] * 2,
        compiler_params=pltpu.CompilerParams(vmem_limit_bytes=16 * 2**20),
        cost_estimate=pl.CostEstimate(
            flops=work * split, bytes_accessed=4 * 2**20, transcendentals=0),
        name="noisy_first",
    )(pairs, den_wa)

    whole_shape = jax.ShapeDtypeStruct((2 * npair + cin // 2 * rows, 2 * cols), BF16)
    strip_shape = jax.ShapeDtypeStruct((cols + cin // 2 * EDGE, 2 * cols), BF16)
    diag_shape = jax.ShapeDtypeStruct((cin // 2 * EDGE + 8, 2 * cols), BF16)
    n_sub_out = 1 if n_sub == 2 else 2
    n_strip_out = 1 if n_strip == 2 else 2
    out_shape = ([strip_shape] + [diag_shape] * n_sub_out) * n_strip_out + [whole_shape] * n_sub_out
    last = npair // 2 - 1
    order = sorted(range(len(blocks)), key=lambda k: (0, 3, 1, 2).index(k))
    packed = pl.pallas_call(
        functools.partial(pack_kernel, geo=geo, order=order),
        grid=(1,),
        out_shape=out_shape,
        in_specs=[
            pl.BlockSpec((2 * pitch, 2 * chans), lambda i: (0, 0)),
            pl.BlockSpec((2 * pitch, 2 * chans), lambda i: (last, 0)),
        ] + [vmem] * (2 + len(blocks)) + [any_spec],
        out_specs=[vmem] * len(out_shape),
        compiler_params=pltpu.CompilerParams(vmem_limit_bytes=8 * 2**20),
        name="pack",
    )(pairs, pairs, left, right, *[blocks[k] for k in order], part_a)

    def up(n):
        return [(i, i - 1) for i in range(1, n)]

    def down(n):
        return [(i, i + 1) for i in range(n - 1)]

    sub_moves = [up(n_sub) + down(n_sub)] if n_sub == 2 else [up(n_sub), down(n_sub)]
    strip_moves = [up(n_strip) + down(n_strip)] if n_strip == 2 else [up(n_strip), down(n_strip)]
    rest, subs = packed[:-n_sub_out], packed[-n_sub_out:]
    sub_in = [lax.ppermute(x, "sub", move) for x, move in zip(subs, sub_moves)]
    diag_in = []
    for k, move in enumerate(strip_moves):
        corners = []
        for n, side in enumerate(sub_moves):
            pairs_of = [(i * n_sub + j, p * n_sub + q) for i, p in move for j, q in side]
            corners.append(lax.ppermute(rest[k * (1 + n_sub_out) + 1 + n], ("strip", "sub"), pairs_of))
        diag_in.append(corners[::-1])
    strip_in = [
        lax.ppermute(rest[k * (1 + n_sub_out)], "strip", move) for k, move in enumerate(strip_moves)]
    got = dict(strip=strip_in[::-1], sub=sub_in[::-1], diag=[x for y in diag_in[::-1] for x in y])
    halos = [x for kind in HALO_ORDER for x in got[kind]]

    part_b, m1, m2, mf, mb = pl.pallas_call(
        functools.partial(second_kernel, geo=geo, skip=split),
        out_shape=[
            jax.ShapeDtypeStruct(((npair - 1 - split) * pitch, 2 * chans), F32),
            jax.ShapeDtypeStruct((3 * 8 * SLOT, 6 * chans), BF16),
            mat, mat, mat,
        ],
        in_specs=[vmem] * 6,
        out_specs=[vmem] * 5,
        compiler_params=pltpu.CompilerParams(vmem_limit_bytes=16 * 2**20),
        cost_estimate=pl.CostEstimate(
            flops=work * (npair - 1 - split), bytes_accessed=8 * 2**20, transcendentals=0),
        name="noisy_second",
    )(pairs, mn, jnp.swapaxes(enc_w1, 1, 2), enc_w2, den_wa, den_wb)
    mats = [m1, m2, mn, mf, mb]

    flat = BASE + (npair + 3) * pitch + 16
    windows = geo["windows"]
    field_scratch = pltpu.VMEM((flat, 2 * chans), BF16)
    edge_scratch = pltpu.VMEM((BASE + 2 * pitch + 16, 2 * chans), BF16)
    cond_scratch = pltpu.VMEM(((6 * windows + 2) * SLOT, cols), F32)
    whole_scratch = pltpu.VMEM((chans, rows, cols), BF16)
    inputs = [part_a, part_b, pairs, pairs, left, right, subs[0], *halos, *mats,
              enc_b1[None], enc_b2[None], den_ba[None], noise_gain[None]]
    in_specs = [vmem] * len(inputs)
    in_specs[2] = pl.BlockSpec((2 * pitch, 2 * chans), lambda i: (0, 0))
    in_specs[3] = pl.BlockSpec((2 * pitch, 2 * chans), lambda i: (last, 0))
    result = pl.pallas_call(
        functools.partial(main_kernel, geo=geo, n_strip_in=n_strip_out, n_sub_in=n_sub_out),
        grid=(1,),
        out_shape=jax.ShapeDtypeStruct((chans, rows, cols), BF16),
        in_specs=[vmem, vmem] + in_specs,
        out_specs=any_spec,
        scratch_shapes=[
            field_scratch, field_scratch, field_scratch,
            edge_scratch, edge_scratch,
            pltpu.VMEM((8 * npair + 16, 2 * chans), BF16),
            pltpu.VMEM((8 * (npair - 1), 2 * chans), F32),
            cond_scratch, cond_scratch,
            pltpu.VMEM((BASE + windows * pitch + 16, 8 * SLOT), BF16),
            whole_scratch,
            pltpu.VMEM((chans * OUT_STRIDE, cols), F32),
            pltpu.SemaphoreType.DMA((-(-npair // 8),)),
        ],
        compiler_params=pltpu.CompilerParams(vmem_limit_bytes=28 * 2**20),
        name="denoise",
    )(scales, field, *inputs)
    return result[None]


def solution(mesh):
    return jax.shard_map(
        local,
        mesh=mesh,
        in_specs=(
            P(("group", "member"), None, "strip", "sub"),
            P("group", ("strip", "member"), "sub"),
            P(("group", "member")),
            P(),
            P(),
            P(),
            P(),
            P(),
            P(),
            P(),
            P(),
        ),
        out_specs=P(("group", "member"), None, "strip", "sub"),
        check_vma=False,
    )
```

```python
import functools
import math

import jax
import jax.numpy as jnp
from jax import lax
from jax.experimental import pallas as pl
from jax.experimental.pallas import tpu as pltpu
from jax.sharding import PartitionSpec as P

LEVELS = 18
SIGMA_DATA = 0.5
SIG_LOW = 0.25
SIG_HIGH = 4.0

BF16 = jnp.bfloat16
F32 = jnp.float32
NT = (((1,), (1,)), ((), ()))
NN = (((1,), (0,)), ((), ()))

BASE = 8
HALO = 4
EDGE = HALO
EARLY = 4
GROUP = 8
OUT_STRIDE = 17
HALO_ORDER = ("strip", "diag", "sub")
TALL = 6


def plan(level_ref):
    level = level_ref[0:1, :]
    sigma = SIG_LOW * jnp.exp(level * (math.log(SIG_HIGH / SIG_LOW) / (LEVELS - 1)))
    spread = sigma * sigma + SIGMA_DATA * SIGMA_DATA
    root = jnp.sqrt(spread)
    return 1.0 / root, SIGMA_DATA * SIGMA_DATA / spread, sigma * SIGMA_DATA / root, jnp.log(sigma) / 4.0


def prep_kernel(level_ref, field_hbm, cond_hbm, pairs_ref, left_ref, right_ref, cond_ref, scale_ref,
                raw, buf, sems, *, pitch):
    steps, chans, tall, cols = raw.shape
    gets = []
    for s in range(steps):
        get = pltpu.make_async_copy(field_hbm.at[:, pl.ds(s * tall, tall), :], raw.at[s], sems.at[s])
        get.start()
        gets.append(get)
    get_cond = pltpu.make_async_copy(cond_hbm, cond_ref, sems.at[steps])
    get_cond.start()
    c_in, c_skip, c_out, c_noise = plan(level_ref)
    scale_ref[...] = jnp.concatenate(
        [c_skip, c_out, c_noise, jnp.zeros((5, 128), F32)], axis=0)
    for s in range(steps):
        gets[s].wait()
        buf[...] = raw[s].astype(F32).reshape(chans * tall, cols)
        for q in range(tall // 2):
            at = s * (tall // 2) + q
            for h in range(2):
                row = buf[pl.ds(2 * q + h, chans, stride=tall), :]
                cells = (c_in * row.T).astype(BF16)
                lanes = slice(h * chans, (h + 1) * chans)
                pairs_ref[at * pitch + 2:at * pitch + 2 + cols, lanes] = cells
                left_ref[2 * at:2 * at + 2, lanes] = cells[:2]
                right_ref[2 * at:2 * at + 2, lanes] = cells[cols - 2:]
    get_cond.wait()


def pack_kernel(*refs, geo, order):
    block_count = len(order)
    top_ref, bottom_ref, left_ref, right_ref = refs[:4]
    blocks = [refs[4 + order.index(k)] for k in range(block_count)]
    outs = list(refs[4 + block_count + 1:])
    n_strip, n_sub, n_member = geo["n_strip"], geo["n_sub"], geo["n_member"]
    pitch, cols, rows, cin = geo["pitch"], geo["cols"], geo["rows"], geo["cin"]
    half = cin // 2
    member = lax.axis_index("member")
    strip = lax.axis_index("strip")
    sub = lax.axis_index("sub")

    n_sub_out = 1 if n_sub == 2 else 2
    rest, subs = outs[:-n_sub_out], outs[-n_sub_out:]
    whole = subs[0]
    for k, block in enumerate(blocks):
        tall = block.shape[1]
        if block_count == 1:
            at = 0
        else:
            at = pl.multiple_of(jnp.bitwise_xor(member, k) * tall, tall)
        for c in range(cin):
            lanes = slice((c // half) * cols, (c // half + 1) * cols)
            start = 2 * (rows // 2) + (c % half) * rows + at
            if block_count != 1:
                start = pl.multiple_of(start, 16)
            whole[pl.ds(start, tall), lanes] = block[c]
    noisy_rows = 2 * (rows // 2)
    whole_left = left_ref[...]
    whole_right = right_ref[...]

    def cond_edge(c, top):
        lanes = slice((c // half) * cols, (c // half + 1) * cols)
        start = noisy_rows + (c % half) * rows
        if top:
            return whole[start:start + EDGE, lanes]
        return whole[start + rows - EDGE:start + rows, lanes]

    def pick(flag, a, b):
        return jnp.where(flag, a.astype(F32), b.astype(F32)).astype(BF16)

    def pair_edge(top):
        if top:
            return top_ref[2:2 + cols, :]
        return bottom_ref[pitch + 2:pitch + 2 + cols, :]

    if n_sub == 2:
        whole[:noisy_rows, :] = pick(sub == 0, whole_right, whole_left)
    else:
        whole[:noisy_rows, :] = whole_left
        other = subs[1]
        other[noisy_rows:, :] = whole[noisy_rows:, :]
        other[:noisy_rows, :] = whole_right
    tops = [None] if n_strip == 2 else [True, False]
    for at, top in enumerate(tops):
        if top is None:
            pair = pick(strip == 0, pair_edge(False), pair_edge(True))
        else:
            pair = pair_edge(top)
        strip_out = rest[at]
        strip_out[:cols, :] = pair
        for c in range(cin):
            lanes = slice((c // half) * cols, (c // half + 1) * cols)
            if top is None:
                cells = pick(strip == 0, cond_edge(c, False), cond_edge(c, True))
            else:
                cells = cond_edge(c, top)
            start = cols + (c % half) * EDGE
            strip_out[start:start + EDGE, lanes] = cells


def corner_kernel(strip_ref, *outs, cols):
    cond_rows = strip_ref.shape[0] - cols
    for out in outs:
        out[:cond_rows, :] = strip_ref[cols:, :]
    if len(outs) == 1:
        first = lax.axis_index("sub") == 0
        cells = jnp.where(first, strip_ref[cols - 2:cols, :].astype(F32), strip_ref[:2, :].astype(F32))
        outs[0][cond_rows:cond_rows + 2, :] = cells.astype(BF16)
    else:
        outs[0][cond_rows:cond_rows + 2, :] = strip_ref[:2, :]
        outs[1][cond_rows:cond_rows + 2, :] = strip_ref[cols - 2:cols, :]


def conv(pieces, weight):
    lo, hi = slice(0, 128), slice(128, 256)

    def rows_of(lanes, shift, extra):
        return jnp.concatenate(
            [src[at + shift(pitch):at + shift(pitch) + span + extra, lanes]
             for src, at, span, pitch in pieces], axis=0)

    inner = []
    for b in range(3):
        inner.append(rows_of(hi, lambda pitch: b, 0))
        inner.append(rows_of(lo, lambda pitch: pitch + b, 0))
    y = lax.dot_general(
        jnp.concatenate(inner, axis=1), weight[:, :768], NT, preferred_element_type=F32)
    upper = jnp.concatenate([rows_of(lo, lambda pitch: b, 8) for b in range(2)], axis=1)
    upper = lax.dot_general(upper, weight[:, 768:1024], NT, preferred_element_type=F32)
    lower = jnp.concatenate([rows_of(hi, lambda pitch: pitch + b, 8) for b in range(2)], axis=1)
    lower = lax.dot_general(lower, weight[:, 1024:], NT, preferred_element_type=F32)
    results = []
    at = more = 0
    for _, _, span, _ in pieces:
        a, b = upper[more:more + span + 8], lower[more:more + span + 8]
        outer = [a[:span, lo] + a[1:span + 1, hi], b[:span, lo] + b[1:span + 1, hi]]
        results.append(y[at:at + span] + jnp.concatenate(outer, axis=1))
        at += span
        more += span + 8
    return results


def tiles_of(dst, src, lanes):
    zero = jnp.zeros((128, 128), BF16)
    tap = [[src[3 * a + b, :, lanes] for b in range(3)] for a in range(3)]

    def put(at, blocks):
        for n in range(2):
            for k in range(2):
                dst[n * 128:(n + 1) * 128, at + k * 128:at + (k + 1) * 128] = blocks[n][k]

    for b in range(3):
        put(b * 256, [[tap[1][b], tap[2][b]], [tap[0][b], tap[1][b]]])
    put(768, [[tap[0][0], tap[0][1]], [zero, tap[0][2]]])
    put(1024, [[tap[2][0], tap[2][1]], [zero, tap[2][2]]])


def chunks(total, size):
    return [(at, min(size, total - at)) for at in range(0, total, size)]


def first_kernel(pairs, wa, part, mn, *, pitch):
    tiles_of(mn, wa, slice(0, 128))
    for first, count in chunks(part.shape[0] // pitch, GROUP):
        part[first * pitch:(first + count) * pitch, :] = conv(
            [(pairs, first * pitch, count * pitch, pitch)], mn)[0]


def second_kernel(pairs, mn, w1, w2, wa, wb, part, m1, m2, mf, mb, *, geo, skip):
    pitch, cin = geo["pitch"], geo["cin"]
    chans = 128
    for first, count in chunks(part.shape[0] // pitch, GROUP):
        part[first * pitch:(first + count) * pitch, :] = conv(
            [(pairs, (skip + first) * pitch, count * pitch, pitch)], mn)[0]
    tiles_of(m2, w2, slice(0, chans))
    tiles_of(mf, wa, slice(chans, 2 * chans))
    tiles_of(mb, wb, slice(0, chans))
    m1[...] = jnp.zeros_like(m1)
    for b in range(3):
        for n in range(TALL - 2):
            for a in range(3):
                at = (b * TALL + n + a) * cin
                m1[at:at + cin, n * chans:(n + 1) * chans] = w1[3 * a + b]


def main_kernel(*refs, geo, n_strip_in, n_sub_in):
    it = iter(refs)
    scales = next(it)
    field = next(it)
    part_a, part_b, pairs_top, pairs_bottom, left, right, own = [next(it) for _ in range(7)]
    split = part_a.shape[0] // geo["pitch"]
    got = {}
    for kind in HALO_ORDER:
        count = dict(strip=n_strip_in, sub=n_sub_in, diag=n_strip_in * n_sub_in)[kind]
        got[kind] = [next(it) for _ in range(count)]
    strip_in, sub_in = got["strip"], got["sub"]
    diag_in = [got["diag"][k * n_sub_in:(k + 1) * n_sub_in] for k in range(n_strip_in)]
    m1, m2, mn, mf, mb, b1, b2, ba, gain = [next(it) for _ in range(9)]
    out_hbm = next(it)
    (xe, xf, xh, xt, xb, xc, yc, cr, ch, lw, out, obuf, sems) = list(it)

    n_strip, n_sub = geo["n_strip"], geo["n_sub"]
    pitch, cols, rows, cin = geo["pitch"], geo["cols"], geo["rows"], geo["cin"]
    chans = 128
    half = cin // 2
    npair = rows // 2
    noisy_rows = 2 * npair
    strip = lax.axis_index("strip")
    sub = lax.axis_index("sub")
    above, below = strip > 0, strip < n_strip - 1
    before, after = sub > 0, sub < n_sub - 1

    c_skip, c_out, c_noise = scales[0:1, :], scales[1:2, :], scales[2:3, :]

    def keep(flag, cells):
        return jnp.where(flag, cells.astype(F32), 0.0)

    strip_top, strip_bottom = strip_in[0], strip_in[-1]
    diag_top, diag_bottom = diag_in[0], diag_in[-1]

    def halo_cells(q):
        return (keep(before, sub_in[0][2 * q:2 * q + 2, :]).astype(BF16),
                keep(after, sub_in[-1][2 * q:2 * q + 2, :]).astype(BF16))

    corner = slice(half * EDGE, half * EDGE + 2)
    strip_rows = (
        (xt, strip_top, diag_top, above, 0, pairs_top[:pitch, :], 0, 1),
        (xb, strip_bottom, diag_bottom, below, 1, pairs_bottom[pitch:, :], npair - 1, 0))
    for dst, source, corners, flag, at, inner, q, inner_at in strip_rows:
        at = BASE + at * pitch
        dst[at + 2:at + 2 + cols, :] = keep(flag, source[:cols, :]).astype(BF16)
        dst[at:at + 2, :] = keep(flag & before, corners[0][corner, :]).astype(BF16)
        dst[at + 2 + cols:at + 4 + cols, :] = keep(flag & after, corners[-1][corner, :]).astype(BF16)
        at = BASE + inner_at * pitch
        dst[at:at + pitch, :] = inner
        dst[at:at + 2, :], dst[at + 2 + cols:at + 4 + cols, :] = halo_cells(q)
    for q in range(npair):
        at = 8 * q
        xc[at:at + 2, :], xc[at + 6:at + 8, :] = halo_cells(q)
        xc[at + 2:at + 4, :] = left[2 * q:2 * q + 2, :]
        xc[at + 4:at + 6, :] = right[2 * q:2 * q + 2, :]
    edge_top, edge_bottom, edge_cols = conv(
        [(xt, BASE, pitch, pitch), (xb, BASE, pitch, pitch), (xc, 0, 8 * (npair - 1), 8)], mn)
    yc[...] = edge_cols

    cr[...] = jnp.zeros_like(cr)
    ch[...] = jnp.zeros_like(ch)

    def lanes_of(c):
        return slice((c // half) * cols, (c // half + 1) * cols)

    def fill(dst, body, tops):
        for c in range(cin):
            at = noisy_rows + (c % half) * rows
            dst[pl.ds(HALO * cin + c, rows, stride=cin), :] = (
                body[at:at + rows, lanes_of(c)].astype(F32))
            for source, flag, is_top, first in tops:
                at = first + (c % half) * EDGE
                cells = source[at:at + EDGE, lanes_of(c)].astype(F32)
                if is_top:
                    dst[pl.ds(c, HALO, stride=cin), :] = keep(flag, cells[EDGE - HALO:])
                else:
                    dst[pl.ds((HALO + rows) * cin + c, HALO, stride=cin), :] = keep(flag, cells[:HALO])

    fill(cr, own, [(strip_top, above, True, cols), (strip_bottom, below, False, cols)])
    windows = geo["windows"]
    step = (TALL - 2) * cin
    for w in range(windows):
        at = BASE - HALO + w * pitch
        lw[at + HALO:at + HALO + cols, :] = cr[step * w:step * w + chans, :].T
    for k in range(n_sub_in):
        fill(ch, sub_in[k], [(diag_top[k], above, True, 0), (diag_bottom[k], below, False, 0)])
        for w in range(windows):
            cells = ch[step * w:step * w + chans, :].T
            at = BASE - HALO + w * pitch
            if k == 0:
                lw[at:at + HALO, :] = keep(before, cells[cols - HALO:])
            if k == n_sub_in - 1:
                lw[at + HALO + cols:at + 2 * HALO + cols, :] = keep(after, cells[:HALO])

    def inside(y, left, right, first, count, low_row):
        y = y.reshape(count, pitch, 2 * chans)
        col = lax.broadcasted_iota(jnp.int32, (count, 8, 2 * chans), 1)
        head = jnp.where((col >= left) | before, y[:, :8], 0.0)
        tail = jnp.where((col < right - (pitch - 8)) | after, y[:, pitch - 8:], 0.0)
        y = jnp.concatenate([head, y[:, 8:pitch - 8], tail], axis=1)
        parts = []
        for i in range(count):
            halves = []
            for h in range(2):
                row = 2 * (first + i) + h - low_row
                cells = y[i, :, h * chans:(h + 1) * chans]
                if row < 0:
                    cells = jnp.where(above, cells, 0.0)
                elif row >= rows:
                    cells = jnp.where(below, cells, 0.0)
                halves.append(cells)
            parts.append(jnp.concatenate(halves, axis=1))
        return parts

    def silu(v):
        return v * (0.5 * jnp.tanh(0.5 * v) + 0.5)

    def twice(v):
        return jnp.concatenate([v, v], axis=1)

    bias1 = twice(b1[...])
    wide = TALL * cin
    lane = lax.broadcasted_iota(jnp.int32, (1, chans), 1)
    per = 5
    for w0 in range(0, windows, per):
        count = min(per, windows - w0)
        span = count * pitch
        at = BASE - HALO + w0 * pitch
        middle = pltpu.roll(lw[at + 1:at + 1 + span, :], wide, 1)
        last = pltpu.roll(lw[at + 2:at + 2 + span, :], 2 * wide - chans, 1)
        lhs = jnp.concatenate(
            [jnp.where(lane < wide, lw[at:at + span, :], middle),
             jnp.where(lane < 2 * wide - chans, middle, last)], axis=1).astype(BF16)
        y = lax.dot_general(lhs, m1[...], NN, preferred_element_type=F32)
        for p in range((TALL - 2) // 2):
            z = silu(y[:, p * 2 * chans:(p + 1) * 2 * chans] + bias1)
            for i in range(count):
                j = (TALL - 2) // 2 * (w0 + i) + p
                if j < npair + 3:
                    cells = inside(z[i * pitch:(i + 1) * pitch], 3, 3 + cols, j, 1, 3)[0]
                    xe[BASE + j * pitch:BASE + (j + 1) * pitch, :] = cells.astype(BF16)

    bias2 = twice(b2[...])
    for first, count in chunks(npair + 2, GROUP):
        y = conv([(xe, BASE + first * pitch, count * pitch, pitch)], m2)[0] + bias2
        parts = inside(y, 2, 2 + cols, first, count, 2)
        for i, cells in enumerate(parts):
            at = BASE + (first + i) * pitch
            xf[at:at + pitch, :] = cells.astype(BF16)

    offset = twice(ba[...] + c_noise * gain[...])
    first_cols = lax.broadcasted_iota(jnp.int32, (8, 2 * chans), 0) < 2
    for first, count in chunks(npair + 1, GROUP):
        y = conv([(xf, BASE + first * pitch, count * pitch, pitch)], mf)[0] + offset
        noisy = []
        for j in range(first, first + count):
            if j == 0:
                noisy.append(edge_top)
            elif j == npair:
                noisy.append(edge_bottom)
            else:
                part, at = (part_a, j - 1) if j - 1 < split else (part_b, j - 1 - split)
                at *= pitch
                edge = yc[8 * (j - 1):8 * j, :]
                noisy.append(jnp.where(first_cols, edge, part[at:at + 8, :]))
                noisy.append(part[at + 8:at + cols, :])
                noisy.append(jnp.where(
                    first_cols, pltpu.roll(edge, 4, 0), part[at + cols:at + cols + 8, :]))
        y = y + jnp.concatenate(noisy, axis=0)
        parts = inside(silu(y), 1, 1 + cols, first, count, 1)
        for i, cells in enumerate(parts):
            at = BASE + (first + i) * pitch
            xh[at:at + pitch, :] = cells.astype(BF16)

    puts = []
    for first, count in chunks(npair, 8):
        y = conv([(xh, BASE + first * pitch, count * pitch, pitch)], mb)[0]
        tall = 2 * count
        for i in range(count):
            for h in range(2):
                cells = y[i * pitch:i * pitch + cols, h * chans:(h + 1) * chans]
                obuf[pl.ds(2 * i + h, chans, stride=OUT_STRIDE), :] = cells.T
        r0 = 2 * first
        for c in range(chans):
            update = obuf[c * OUT_STRIDE:c * OUT_STRIDE + tall, :]
            skip = field[c, r0:r0 + tall, :].astype(F32)
            out[c, r0:r0 + tall, :] = (c_skip * skip + c_out * update).astype(BF16)
        put = pltpu.make_async_copy(
            out.at[:, pl.ds(r0, tall), :], out_hbm.at[:, pl.ds(r0, tall), :],
            sems.at[first // 8])
        put.start()
        puts.append(put)
    for put in puts:
        put.wait()


def local(
    noisy, condition, levels, enc_w1, enc_b1, enc_w2, enc_b2, den_wa, den_ba, noise_gain, den_wb
):
    field = noisy[0]
    chans, rows, cols = field.shape
    cin = condition.shape[0]
    n_member = lax.axis_size("member")
    n_strip = lax.axis_size("strip")
    n_sub = lax.axis_size("sub")
    pitch = cols + 2 * HALO
    npair = rows // 2
    geo = dict(n_strip=n_strip, n_sub=n_sub, n_member=n_member, pitch=pitch, cols=cols, rows=rows,
               cin=cin, windows=-(-(rows + 6) // (TALL - 2)))

    if n_member in (1, 2, 4):
        blocks = [condition]
        for k in range(1, n_member):
            blocks.append(
                lax.ppermute(condition, "member", [(i, i ^ k) for i in range(n_member)]))
    else:
        blocks = [lax.all_gather(condition, "member", axis=1, tiled=True)]

    tall = 16
    steps = rows // tall
    any_spec = pl.BlockSpec(memory_space=pl.ANY)
    vmem = pl.BlockSpec(memory_space=pltpu.VMEM)
    pairs, left, right, own_cond, scales = pl.pallas_call(
        functools.partial(prep_kernel, pitch=pitch),
        out_shape=[
            jax.ShapeDtypeStruct((npair * pitch + 16, 2 * chans), BF16),
            jax.ShapeDtypeStruct((2 * npair, 2 * chans), BF16),
            jax.ShapeDtypeStruct((2 * npair, 2 * chans), BF16),
            jax.ShapeDtypeStruct(condition.shape, BF16),
            jax.ShapeDtypeStruct((8, 128), F32),
        ],
        in_specs=[vmem] + [pl.BlockSpec(memory_space=pltpu.HBM)] * 2,
        out_specs=[vmem] * 5,
        scratch_shapes=[
            pltpu.VMEM((steps, chans, tall, cols), BF16),
            pltpu.VMEM((chans * tall, cols), F32),
            pltpu.SemaphoreType.DMA((steps + 1,)),
        ],
        compiler_params=pltpu.CompilerParams(vmem_limit_bytes=12 * 2**20),
        cost_estimate=pl.CostEstimate(flops=0, bytes_accessed=16 * 2**20, transcendentals=0),
        name="prep",
    )(jnp.broadcast_to(levels.astype(F32)[:, None], (8, 128)), *[pltpu.with_memory_space_constraint(x, pltpu.HBM) for x in (field, condition)])
    if len(blocks) > 1:
        blocks[0] = own_cond

    mat = jax.ShapeDtypeStruct((2 * chans, 10 * chans), BF16)
    work = 2 * 9 * chans * chans * 2 * cols
    split = EARLY
    part_a, mn = pl.pallas_call(
        functools.partial(first_kernel, pitch=pitch),
        out_shape=[jax.ShapeDtypeStruct((split * pitch, 2 * chans), F32), mat],
        in_specs=[vmem] * 2,
        out_specs=[vmem] * 2,
        compiler_params=pltpu.CompilerParams(vmem_limit_bytes=16 * 2**20),
        cost_estimate=pl.CostEstimate(
            flops=work * split, bytes_accessed=4 * 2**20, transcendentals=0),
        name="noisy_first",
    )(pairs, den_wa)

    whole_shape = jax.ShapeDtypeStruct((2 * npair + cin // 2 * rows, 2 * cols), BF16)
    strip_shape = jax.ShapeDtypeStruct((cols + cin // 2 * EDGE, 2 * cols), BF16)
    diag_shape = jax.ShapeDtypeStruct((cin // 2 * EDGE + 8, 2 * cols), BF16)
    n_sub_out = 1 if n_sub == 2 else 2
    n_strip_out = 1 if n_strip == 2 else 2
    out_shape = [strip_shape] * n_strip_out + [whole_shape] * n_sub_out
    last = npair // 2 - 1
    order = sorted(range(len(blocks)), key=lambda k: (0, 3, 1, 2).index(k))
    packed = pl.pallas_call(
        functools.partial(pack_kernel, geo=geo, order=order),
        grid=(1,),
        out_shape=out_shape,
        in_specs=[
            pl.BlockSpec((2 * pitch, 2 * chans), lambda i: (0, 0)),
            pl.BlockSpec((2 * pitch, 2 * chans), lambda i: (last, 0)),
        ] + [vmem] * (2 + len(blocks)) + [any_spec],
        out_specs=[vmem] * len(out_shape),
        compiler_params=pltpu.CompilerParams(vmem_limit_bytes=8 * 2**20),
        name="pack",
    )(pairs, pairs, left, right, *[blocks[k] for k in order], part_a)

    def up(n):
        return [(i, i - 1) for i in range(1, n)]

    def down(n):
        return [(i, i + 1) for i in range(n - 1)]

    sub_moves = [up(n_sub) + down(n_sub)] if n_sub == 2 else [up(n_sub), down(n_sub)]
    strip_moves = [up(n_strip) + down(n_strip)] if n_strip == 2 else [up(n_strip), down(n_strip)]
    strips, subs = packed[:-n_sub_out], packed[-n_sub_out:]
    diags = [
        pl.pallas_call(
            functools.partial(corner_kernel, cols=cols),
            out_shape=[diag_shape] * n_sub_out,
            in_specs=[vmem],
            out_specs=[vmem] * n_sub_out,
            compiler_params=pltpu.CompilerParams(vmem_limit_bytes=8 * 2**20),
            name="corners",
        )(strip)
        for strip in strips
    ]
    sub_in = [lax.ppermute(x, "sub", move) for x, move in zip(subs, sub_moves)]
    diag_in = []
    for k, move in enumerate(strip_moves):
        corners = []
        for n, side in enumerate(sub_moves):
            pairs_of = [(i * n_sub + j, p * n_sub + q) for i, p in move for j, q in side]
            corners.append(lax.ppermute(diags[k][n], ("strip", "sub"), pairs_of))
        diag_in.append(corners[::-1])
    strip_in = [lax.ppermute(x, "strip", move) for x, move in zip(strips, strip_moves)]
    got = dict(strip=strip_in[::-1], sub=sub_in[::-1], diag=[x for y in diag_in[::-1] for x in y])
    halos = [x for kind in HALO_ORDER for x in got[kind]]

    part_b, m1, m2, mf, mb = pl.pallas_call(
        functools.partial(second_kernel, geo=geo, skip=split),
        out_shape=[
            jax.ShapeDtypeStruct(((npair - 1 - split) * pitch, 2 * chans), F32),
            jax.ShapeDtypeStruct((2 * chans, (TALL - 2) * chans), BF16),
            mat, mat, mat,
        ],
        in_specs=[vmem] * 6,
        out_specs=[vmem] * 5,
        compiler_params=pltpu.CompilerParams(vmem_limit_bytes=16 * 2**20),
        cost_estimate=pl.CostEstimate(
            flops=work * (npair - 1 - split), bytes_accessed=8 * 2**20, transcendentals=0),
        name="noisy_second",
    )(pairs, mn, jnp.swapaxes(enc_w1, 1, 2), enc_w2, den_wa, den_wb)
    mats = [m1, m2, mn, mf, mb]

    flat = BASE + (npair + 3) * pitch + 16
    windows = geo["windows"]
    field_scratch = pltpu.VMEM((flat, 2 * chans), BF16)
    edge_scratch = pltpu.VMEM((BASE + 2 * pitch + 16, 2 * chans), BF16)
    cond_scratch = pltpu.VMEM(((TALL - 2) * cin * (windows - 1) + chans, cols), F32)
    whole_scratch = pltpu.VMEM((chans, rows, cols), BF16)
    inputs = [part_a, part_b, pairs, pairs, left, right, subs[0], *halos, *mats,
              enc_b1[None], enc_b2[None], den_ba[None], noise_gain[None]]
    in_specs = [vmem] * len(inputs)
    in_specs[2] = pl.BlockSpec((2 * pitch, 2 * chans), lambda i: (0, 0))
    in_specs[3] = pl.BlockSpec((2 * pitch, 2 * chans), lambda i: (last, 0))
    result = pl.pallas_call(
        functools.partial(main_kernel, geo=geo, n_strip_in=n_strip_out, n_sub_in=n_sub_out),
        grid=(1,),
        out_shape=jax.ShapeDtypeStruct((chans, rows, cols), BF16),
        in_specs=[vmem, vmem] + in_specs,
        out_specs=any_spec,
        scratch_shapes=[
            field_scratch, field_scratch, field_scratch,
            edge_scratch, edge_scratch,
            pltpu.VMEM((8 * npair + 16, 2 * chans), BF16),
            pltpu.VMEM((8 * (npair - 1), 2 * chans), F32),
            cond_scratch, cond_scratch,
            pltpu.VMEM((BASE + windows * pitch + 16, chans), F32),
            whole_scratch,
            pltpu.VMEM((chans * OUT_STRIDE, cols), F32),
            pltpu.SemaphoreType.DMA((-(-npair // 8),)),
        ],
        compiler_params=pltpu.CompilerParams(vmem_limit_bytes=28 * 2**20),
        name="denoise",
    )(scales, field, *inputs)
    return result[None]


def solution(mesh):
    return jax.shard_map(
        local,
        mesh=mesh,
        in_specs=(
            P(("group", "member"), None, "strip", "sub"),
            P("group", ("strip", "member"), "sub"),
            P(("group", "member")),
            P(),
            P(),
            P(),
            P(),
            P(),
            P(),
            P(),
            P(),
        ),
        out_specs=P(("group", "member"), None, "strip", "sub"),
        check_vma=False,
    )
```

```python
import functools
import math

import jax
import jax.numpy as jnp
from jax import lax
from jax.experimental import pallas as pl
from jax.experimental.pallas import tpu as pltpu
from jax.sharding import PartitionSpec as P

LEVELS = 18
SIGMA_DATA = 0.5
SIG_LOW = 0.25
SIG_HIGH = 4.0

BF16 = jnp.bfloat16
F32 = jnp.float32
NT = (((1,), (1,)), ((), ()))
NN = (((1,), (0,)), ((), ()))

BASE = 8
HALO = 4
EDGE = HALO
EARLY = 4
GROUP = 8
OUT_STRIDE = 17
HALO_ORDER = ("strip", "diag", "sub")
TALL = 6


def plan(level_ref):
    level = level_ref[0:1, :]
    sigma = SIG_LOW * jnp.exp(level * (math.log(SIG_HIGH / SIG_LOW) / (LEVELS - 1)))
    spread = sigma * sigma + SIGMA_DATA * SIGMA_DATA
    root = jnp.sqrt(spread)
    return 1.0 / root, SIGMA_DATA * SIGMA_DATA / spread, sigma * SIGMA_DATA / root, jnp.log(sigma) / 4.0


def prep_kernel(level_ref, field_hbm, cond_hbm, pairs_ref, left_ref, right_ref, cond_ref, scale_ref,
                raw, buf, sems, *, pitch):
    steps, chans, tall, cols = raw.shape
    gets = []
    for s in range(steps):
        get = pltpu.make_async_copy(field_hbm.at[:, pl.ds(s * tall, tall), :], raw.at[s], sems.at[s])
        get.start()
        gets.append(get)
    get_cond = pltpu.make_async_copy(cond_hbm, cond_ref, sems.at[steps])
    get_cond.start()
    c_in, c_skip, c_out, c_noise = plan(level_ref)
    scale_ref[...] = jnp.concatenate(
        [c_skip, c_out, c_noise, jnp.zeros((5, 128), F32)], axis=0)
    for s in range(steps):
        gets[s].wait()
        buf[...] = raw[s].astype(F32).reshape(chans * tall, cols)
        for q in range(tall // 2):
            at = s * (tall // 2) + q
            for h in range(2):
                row = buf[pl.ds(2 * q + h, chans, stride=tall), :]
                cells = (c_in * row.T).astype(BF16)
                lanes = slice(h * chans, (h + 1) * chans)
                pairs_ref[at * pitch + 2:at * pitch + 2 + cols, lanes] = cells
                left_ref[2 * at:2 * at + 2, lanes] = cells[:2]
                right_ref[2 * at:2 * at + 2, lanes] = cells[cols - 2:]
    get_cond.wait()


def pack_kernel(*refs, geo, order):
    block_count = len(order)
    top_ref, bottom_ref, left_ref, right_ref = refs[:4]
    blocks = [refs[4 + order.index(k)] for k in range(block_count)]
    outs = list(refs[4 + block_count + 1:])
    n_strip, n_sub, n_member = geo["n_strip"], geo["n_sub"], geo["n_member"]
    pitch, cols, rows, cin = geo["pitch"], geo["cols"], geo["rows"], geo["cin"]
    half = cin // 2
    member = lax.axis_index("member")
    strip = lax.axis_index("strip")
    sub = lax.axis_index("sub")

    n_sub_out = 1 if n_sub == 2 else 2
    rest, subs = outs[:-n_sub_out], outs[-n_sub_out:]
    whole = subs[0]
    for k, block in enumerate(blocks):
        tall = block.shape[1]
        if block_count == 1:
            at = 0
        else:
            at = pl.multiple_of(jnp.bitwise_xor(member, k) * tall, tall)
        for c in range(cin):
            lanes = slice((c // half) * cols, (c // half + 1) * cols)
            start = 2 * (rows // 2) + (c % half) * rows + at
            if block_count != 1:
                start = pl.multiple_of(start, 16)
            whole[pl.ds(start, tall), lanes] = block[c]
    noisy_rows = 2 * (rows // 2)
    whole_left = left_ref[...]
    whole_right = right_ref[...]

    def cond_edge(c, top):
        lanes = slice((c // half) * cols, (c // half + 1) * cols)
        start = noisy_rows + (c % half) * rows
        if top:
            return whole[start:start + EDGE, lanes]
        return whole[start + rows - EDGE:start + rows, lanes]

    def pick(flag, a, b):
        return jnp.where(flag, a.astype(F32), b.astype(F32)).astype(BF16)

    def pair_edge(top):
        if top:
            return top_ref[2:2 + cols, :]
        return bottom_ref[pitch + 2:pitch + 2 + cols, :]

    if n_sub == 2:
        whole[:noisy_rows, :] = pick(sub == 0, whole_right, whole_left)
    else:
        whole[:noisy_rows, :] = whole_left
        other = subs[1]
        other[noisy_rows:, :] = whole[noisy_rows:, :]
        other[:noisy_rows, :] = whole_right
    tops = [None] if n_strip == 2 else [True, False]
    for at, top in enumerate(tops):
        if top is None:
            pair = pick(strip == 0, pair_edge(False), pair_edge(True))
        else:
            pair = pair_edge(top)
        strip_out = rest[at]
        strip_out[:cols, :] = pair
        for c in range(cin):
            lanes = slice((c // half) * cols, (c // half + 1) * cols)
            if top is None:
                cells = pick(strip == 0, cond_edge(c, False), cond_edge(c, True))
            else:
                cells = cond_edge(c, top)
            start = cols + (c % half) * EDGE
            strip_out[start:start + EDGE, lanes] = cells


def corner_kernel(strip_ref, *outs, cols):
    cond_rows = strip_ref.shape[0] - cols
    for out in outs:
        out[:cond_rows, :] = strip_ref[cols:, :]
    if len(outs) == 1:
        first = lax.axis_index("sub") == 0
        cells = jnp.where(first, strip_ref[cols - 2:cols, :].astype(F32), strip_ref[:2, :].astype(F32))
        outs[0][cond_rows:cond_rows + 2, :] = cells.astype(BF16)
    else:
        outs[0][cond_rows:cond_rows + 2, :] = strip_ref[:2, :]
        outs[1][cond_rows:cond_rows + 2, :] = strip_ref[cols - 2:cols, :]


def conv(pieces, weight):
    lo, hi = slice(0, 128), slice(128, 256)

    def rows_of(lanes, shift, extra):
        return jnp.concatenate(
            [src[at + shift(pitch):at + shift(pitch) + span + extra, lanes]
             for src, at, span, pitch in pieces], axis=0)

    inner = []
    for b in range(3):
        inner.append(rows_of(hi, lambda pitch: b, 0))
        inner.append(rows_of(lo, lambda pitch: pitch + b, 0))
    y = lax.dot_general(
        jnp.concatenate(inner, axis=1), weight[:, :768], NT, preferred_element_type=F32)
    upper = jnp.concatenate([rows_of(lo, lambda pitch: b, 8) for b in range(2)], axis=1)
    upper = lax.dot_general(upper, weight[:, 768:1024], NT, preferred_element_type=F32)
    lower = jnp.concatenate([rows_of(hi, lambda pitch: pitch + b, 8) for b in range(2)], axis=1)
    lower = lax.dot_general(lower, weight[:, 1024:], NT, preferred_element_type=F32)
    results = []
    at = more = 0
    for _, _, span, _ in pieces:
        a, b = upper[more:more + span + 8], lower[more:more + span + 8]
        outer = [a[:span, lo] + a[1:span + 1, hi], b[:span, lo] + b[1:span + 1, hi]]
        results.append(y[at:at + span] + jnp.concatenate(outer, axis=1))
        at += span
        more += span + 8
    return results


def tiles_of(dst, src, lanes):
    zero = jnp.zeros((128, 128), BF16)
    tap = [[src[3 * a + b, :, lanes] for b in range(3)] for a in range(3)]

    def put(at, blocks):
        for n in range(2):
            for k in range(2):
                dst[n * 128:(n + 1) * 128, at + k * 128:at + (k + 1) * 128] = blocks[n][k]

    for b in range(3):
        put(b * 256, [[tap[1][b], tap[2][b]], [tap[0][b], tap[1][b]]])
    put(768, [[tap[0][0], tap[0][1]], [zero, tap[0][2]]])
    put(1024, [[tap[2][0], tap[2][1]], [zero, tap[2][2]]])


def chunks(total, size):
    return [(at, min(size, total - at)) for at in range(0, total, size)]


def first_kernel(pairs, wa, part, mn, *, pitch):
    tiles_of(mn, wa, slice(0, 128))
    for first, count in chunks(part.shape[0] // pitch, GROUP):
        part[first * pitch:(first + count) * pitch, :] = conv(
            [(pairs, first * pitch, count * pitch, pitch)], mn)[0]


def second_kernel(pairs, mn, w1, w2, wa, wb, part, m1, m2, mf, mb, *, geo, skip):
    pitch, cin = geo["pitch"], geo["cin"]
    chans = 128
    for first, count in chunks(part.shape[0] // pitch, GROUP):
        part[first * pitch:(first + count) * pitch, :] = conv(
            [(pairs, (skip + first) * pitch, count * pitch, pitch)], mn)[0]
    tiles_of(m2, w2, slice(0, chans))
    tiles_of(mf, wa, slice(chans, 2 * chans))
    tiles_of(mb, wb, slice(0, chans))
    m1[...] = jnp.zeros_like(m1)
    for b in range(3):
        for n in range(TALL - 2):
            for a in range(3):
                at = (b * TALL + n + a) * cin
                m1[at:at + cin, n * chans:(n + 1) * chans] = w1[3 * a + b]


def main_kernel(*refs, geo, n_strip_in, n_sub_in):
    it = iter(refs)
    scales = next(it)
    field = next(it)
    part_a, part_b, pairs_top, pairs_bottom, left, right, own = [next(it) for _ in range(7)]
    split = part_a.shape[0] // geo["pitch"]
    got = {}
    for kind in HALO_ORDER:
        count = dict(strip=n_strip_in, sub=n_sub_in, diag=n_strip_in * n_sub_in)[kind]
        got[kind] = [next(it) for _ in range(count)]
    strip_in, sub_in = got["strip"], got["sub"]
    diag_in = [got["diag"][k * n_sub_in:(k + 1) * n_sub_in] for k in range(n_strip_in)]
    m1, m2, mn, mf, mb, b1, b2, ba, gain = [next(it) for _ in range(9)]
    out_hbm = next(it)
    (xe, xf, xh, xt, xb, xc, yc, cr, ch, lw, out, obuf, sems) = list(it)

    n_strip, n_sub = geo["n_strip"], geo["n_sub"]
    pitch, cols, rows, cin = geo["pitch"], geo["cols"], geo["rows"], geo["cin"]
    chans = 128
    half = cin // 2
    npair = rows // 2
    noisy_rows = 2 * npair
    strip = lax.axis_index("strip")
    sub = lax.axis_index("sub")
    above, below = strip > 0, strip < n_strip - 1
    before, after = sub > 0, sub < n_sub - 1

    c_skip, c_out, c_noise = scales[0:1, :], scales[1:2, :], scales[2:3, :]

    def keep(flag, cells):
        return jnp.where(flag, cells.astype(F32), 0.0)

    strip_top, strip_bottom = strip_in[0], strip_in[-1]
    diag_top, diag_bottom = diag_in[0], diag_in[-1]

    def halo_cells(q):
        return (keep(before, sub_in[0][2 * q:2 * q + 2, :]).astype(BF16),
                keep(after, sub_in[-1][2 * q:2 * q + 2, :]).astype(BF16))

    corner = slice(half * EDGE, half * EDGE + 2)
    strip_rows = (
        (xt, strip_top, diag_top, above, 0, pairs_top[:pitch, :], 0, 1),
        (xb, strip_bottom, diag_bottom, below, 1, pairs_bottom[pitch:, :], npair - 1, 0))
    for dst, source, corners, flag, at, inner, q, inner_at in strip_rows:
        at = BASE + at * pitch
        dst[at + 2:at + 2 + cols, :] = keep(flag, source[:cols, :]).astype(BF16)
        dst[at:at + 2, :] = keep(flag & before, corners[0][corner, :]).astype(BF16)
        dst[at + 2 + cols:at + 4 + cols, :] = keep(flag & after, corners[-1][corner, :]).astype(BF16)
        at = BASE + inner_at * pitch
        dst[at:at + pitch, :] = inner
        dst[at:at + 2, :], dst[at + 2 + cols:at + 4 + cols, :] = halo_cells(q)
    for q in range(npair):
        at = 8 * q
        xc[at:at + 2, :], xc[at + 6:at + 8, :] = halo_cells(q)
        xc[at + 2:at + 4, :] = left[2 * q:2 * q + 2, :]
        xc[at + 4:at + 6, :] = right[2 * q:2 * q + 2, :]
    edge_top, edge_bottom, edge_cols = conv(
        [(xt, BASE, pitch, pitch), (xb, BASE, pitch, pitch), (xc, 0, 8 * (npair - 1), 8)], mn)
    yc[...] = edge_cols

    cr[...] = jnp.zeros_like(cr)
    ch[...] = jnp.zeros_like(ch)

    def lanes_of(c):
        return slice((c // half) * cols, (c // half + 1) * cols)

    def fill(dst, body, tops):
        for c in range(cin):
            at = noisy_rows + (c % half) * rows
            dst[pl.ds(HALO * cin + c, rows, stride=cin), :] = (
                body[at:at + rows, lanes_of(c)].astype(F32))
            for source, flag, is_top, first in tops:
                at = first + (c % half) * EDGE
                cells = source[at:at + EDGE, lanes_of(c)].astype(F32)
                if is_top:
                    dst[pl.ds(c, HALO, stride=cin), :] = keep(flag, cells[EDGE - HALO:])
                else:
                    dst[pl.ds((HALO + rows) * cin + c, HALO, stride=cin), :] = keep(flag, cells[:HALO])

    fill(cr, own, [(strip_top, above, True, cols), (strip_bottom, below, False, cols)])
    windows = geo["windows"]
    step = (TALL - 2) * cin
    for w in range(windows):
        at = BASE - HALO + w * pitch
        lw[at + HALO:at + HALO + cols, :] = cr[step * w:step * w + chans, :].T
    for k in range(n_sub_in):
        fill(ch, sub_in[k], [(diag_top[k], above, True, 0), (diag_bottom[k], below, False, 0)])
        for w in range(windows):
            cells = ch[step * w:step * w + chans, :].T
            at = BASE - HALO + w * pitch
            if k == 0:
                lw[at:at + HALO, :] = keep(before, cells[cols - HALO:])
            if k == n_sub_in - 1:
                lw[at + HALO + cols:at + 2 * HALO + cols, :] = keep(after, cells[:HALO])

    def inside(y, left, right, first, count, low_row):
        y = y.reshape(count, pitch, 2 * chans)
        col = lax.broadcasted_iota(jnp.int32, (count, 8, 2 * chans), 1)
        head = jnp.where((col >= left) | before, y[:, :8], 0.0)
        tail = jnp.where((col < right - (pitch - 8)) | after, y[:, pitch - 8:], 0.0)
        y = jnp.concatenate([head, y[:, 8:pitch - 8], tail], axis=1)
        parts = []
        for i in range(count):
            halves = []
            for h in range(2):
                row = 2 * (first + i) + h - low_row
                cells = y[i, :, h * chans:(h + 1) * chans]
                if row < 0:
                    cells = jnp.where(above, cells, 0.0)
                elif row >= rows:
                    cells = jnp.where(below, cells, 0.0)
                halves.append(cells)
            parts.append(jnp.concatenate(halves, axis=1))
        return parts

    def silu(v):
        return v * jax.nn.sigmoid(v)

    def twice(v):
        return jnp.concatenate([v, v], axis=1)

    bias1 = twice(b1[...])
    wide = TALL * cin
    lane = lax.broadcasted_iota(jnp.int32, (1, chans), 1)
    per = 5
    for w0 in range(0, windows, per):
        count = min(per, windows - w0)
        span = count * pitch
        at = BASE - HALO + w0 * pitch
        middle = pltpu.roll(lw[at + 1:at + 1 + span, :], wide, 1)
        last = pltpu.roll(lw[at + 2:at + 2 + span, :], 2 * wide - chans, 1)
        lhs = jnp.concatenate(
            [jnp.where(lane < wide, lw[at:at + span, :], middle),
             jnp.where(lane < 2 * wide - chans, middle, last)], axis=1).astype(BF16)
        y = lax.dot_general(lhs, m1[...], NN, preferred_element_type=F32)
        for p in range((TALL - 2) // 2):
            z = silu(y[:, p * 2 * chans:(p + 1) * 2 * chans] + bias1)
            for i in range(count):
                j = (TALL - 2) // 2 * (w0 + i) + p
                if j < npair + 3:
                    cells = inside(z[i * pitch:(i + 1) * pitch], 3, 3 + cols, j, 1, 3)[0]
                    xe[BASE + j * pitch:BASE + (j + 1) * pitch, :] = cells.astype(BF16)

    bias2 = twice(b2[...])
    for first, count in chunks(npair + 2, GROUP):
        y = conv([(xe, BASE + first * pitch, count * pitch, pitch)], m2)[0] + bias2
        parts = inside(y, 2, 2 + cols, first, count, 2)
        for i, cells in enumerate(parts):
            at = BASE + (first + i) * pitch
            xf[at:at + pitch, :] = cells.astype(BF16)

    offset = twice(ba[...] + c_noise * gain[...])
    first_cols = lax.broadcasted_iota(jnp.int32, (8, 2 * chans), 0) < 2
    for first, count in chunks(npair + 1, GROUP):
        y = conv([(xf, BASE + first * pitch, count * pitch, pitch)], mf)[0] + offset
        noisy = []
        for j in range(first, first + count):
            if j == 0:
                noisy.append(edge_top)
            elif j == npair:
                noisy.append(edge_bottom)
            else:
                part, at = (part_a, j - 1) if j - 1 < split else (part_b, j - 1 - split)
                at *= pitch
                edge = yc[8 * (j - 1):8 * j, :]
                noisy.append(jnp.where(first_cols, edge, part[at:at + 8, :]))
                noisy.append(part[at + 8:at + cols, :])
                noisy.append(jnp.where(
                    first_cols, pltpu.roll(edge, 4, 0), part[at + cols:at + cols + 8, :]))
        y = y + jnp.concatenate(noisy, axis=0)
        parts = inside(silu(y), 1, 1 + cols, first, count, 1)
        for i, cells in enumerate(parts):
            at = BASE + (first + i) * pitch
            xh[at:at + pitch, :] = cells.astype(BF16)

    puts = []
    for first, count in chunks(npair, 8):
        y = conv([(xh, BASE + j * pitch, cols, pitch) for j in range(first, first + count)], mb)
        tall = 2 * count
        for i in range(count):
            for h in range(2):
                cells = y[i][:, h * chans:(h + 1) * chans]
                obuf[pl.ds(2 * i + h, chans, stride=OUT_STRIDE), :] = cells.T
        r0 = 2 * first
        for c in range(chans):
            update = obuf[c * OUT_STRIDE:c * OUT_STRIDE + tall, :]
            skip = field[c, r0:r0 + tall, :].astype(F32)
            out[c, r0:r0 + tall, :] = (c_skip * skip + c_out * update).astype(BF16)
        put = pltpu.make_async_copy(
            out.at[:, pl.ds(r0, tall), :], out_hbm.at[:, pl.ds(r0, tall), :],
            sems.at[first // 8])
        put.start()
        puts.append(put)
    for put in puts:
        put.wait()


def local(
    noisy, condition, levels, enc_w1, enc_b1, enc_w2, enc_b2, den_wa, den_ba, noise_gain, den_wb
):
    field = noisy[0]
    chans, rows, cols = field.shape
    cin = condition.shape[0]
    n_member = lax.axis_size("member")
    n_strip = lax.axis_size("strip")
    n_sub = lax.axis_size("sub")
    pitch = cols + 2 * HALO
    npair = rows // 2
    geo = dict(n_strip=n_strip, n_sub=n_sub, n_member=n_member, pitch=pitch, cols=cols, rows=rows,
               cin=cin, windows=-(-(rows + 6) // (TALL - 2)))

    if n_member in (1, 2, 4):
        blocks = [condition]
        for k in range(1, n_member):
            blocks.append(
                lax.ppermute(condition, "member", [(i, i ^ k) for i in range(n_member)]))
    else:
        blocks = [lax.all_gather(condition, "member", axis=1, tiled=True)]

    tall = 16
    steps = rows // tall
    any_spec = pl.BlockSpec(memory_space=pl.ANY)
    vmem = pl.BlockSpec(memory_space=pltpu.VMEM)
    pairs, left, right, own_cond, scales = pl.pallas_call(
        functools.partial(prep_kernel, pitch=pitch),
        out_shape=[
            jax.ShapeDtypeStruct((npair * pitch + 16, 2 * chans), BF16),
            jax.ShapeDtypeStruct((2 * npair, 2 * chans), BF16),
            jax.ShapeDtypeStruct((2 * npair, 2 * chans), BF16),
            jax.ShapeDtypeStruct(condition.shape, BF16),
            jax.ShapeDtypeStruct((8, 128), F32),
        ],
        in_specs=[vmem] + [pl.BlockSpec(memory_space=pltpu.HBM)] * 2,
        out_specs=[vmem] * 5,
        scratch_shapes=[
            pltpu.VMEM((steps, chans, tall, cols), BF16),
            pltpu.VMEM((chans * tall, cols), F32),
            pltpu.SemaphoreType.DMA((steps + 1,)),
        ],
        compiler_params=pltpu.CompilerParams(vmem_limit_bytes=12 * 2**20),
        cost_estimate=pl.CostEstimate(flops=0, bytes_accessed=16 * 2**20, transcendentals=0),
        name="prep",
    )(jnp.broadcast_to(levels.astype(F32)[:, None], (8, 128)), *[pltpu.with_memory_space_constraint(x, pltpu.HBM) for x in (field, condition)])
    if len(blocks) > 1:
        blocks[0] = own_cond

    mat = jax.ShapeDtypeStruct((2 * chans, 10 * chans), BF16)
    work = 2 * 9 * chans * chans * 2 * cols
    split = EARLY
    part_a, mn = pl.pallas_call(
        functools.partial(first_kernel, pitch=pitch),
        out_shape=[jax.ShapeDtypeStruct((split * pitch, 2 * chans), F32), mat],
        in_specs=[vmem] * 2,
        out_specs=[vmem] * 2,
        compiler_params=pltpu.CompilerParams(vmem_limit_bytes=16 * 2**20),
        cost_estimate=pl.CostEstimate(
            flops=work * split, bytes_accessed=4 * 2**20, transcendentals=0),
        name="noisy_first",
    )(pairs, den_wa)

    whole_shape = jax.ShapeDtypeStruct((2 * npair + cin // 2 * rows, 2 * cols), BF16)
    strip_shape = jax.ShapeDtypeStruct((cols + cin // 2 * EDGE, 2 * cols), BF16)
    diag_shape = jax.ShapeDtypeStruct((cin // 2 * EDGE + 8, 2 * cols), BF16)
    n_sub_out = 1 if n_sub == 2 else 2
    n_strip_out = 1 if n_strip == 2 else 2
    out_shape = [strip_shape] * n_strip_out + [whole_shape] * n_sub_out
    last = npair // 2 - 1
    order = sorted(range(len(blocks)), key=lambda k: (0, 3, 1, 2).index(k))
    packed = pl.pallas_call(
        functools.partial(pack_kernel, geo=geo, order=order),
        grid=(1,),
        out_shape=out_shape,
        in_specs=[
            pl.BlockSpec((2 * pitch, 2 * chans), lambda i: (0, 0)),
            pl.BlockSpec((2 * pitch, 2 * chans), lambda i: (last, 0)),
        ] + [vmem] * (2 + len(blocks)) + [any_spec],
        out_specs=[vmem] * len(out_shape),
        compiler_params=pltpu.CompilerParams(vmem_limit_bytes=8 * 2**20),
        name="pack",
    )(pairs, pairs, left, right, *[blocks[k] for k in order], part_a)

    def up(n):
        return [(i, i - 1) for i in range(1, n)]

    def down(n):
        return [(i, i + 1) for i in range(n - 1)]

    sub_moves = [up(n_sub) + down(n_sub)] if n_sub == 2 else [up(n_sub), down(n_sub)]
    strip_moves = [up(n_strip) + down(n_strip)] if n_strip == 2 else [up(n_strip), down(n_strip)]
    strips, subs = packed[:-n_sub_out], packed[-n_sub_out:]
    diags = [
        pl.pallas_call(
            functools.partial(corner_kernel, cols=cols),
            out_shape=[diag_shape] * n_sub_out,
            in_specs=[vmem],
            out_specs=[vmem] * n_sub_out,
            compiler_params=pltpu.CompilerParams(vmem_limit_bytes=8 * 2**20),
            name="corners",
        )(strip)
        for strip in strips
    ]
    sub_in = [lax.ppermute(x, "sub", move) for x, move in zip(subs, sub_moves)]
    diag_in = []
    for k, move in enumerate(strip_moves):
        corners = []
        for n, side in enumerate(sub_moves):
            pairs_of = [(i * n_sub + j, p * n_sub + q) for i, p in move for j, q in side]
            corners.append(lax.ppermute(diags[k][n], ("strip", "sub"), pairs_of))
        diag_in.append(corners[::-1])
    strip_in = [lax.ppermute(x, "strip", move) for x, move in zip(strips, strip_moves)]
    got = dict(strip=strip_in[::-1], sub=sub_in[::-1], diag=[x for y in diag_in[::-1] for x in y])
    halos = [x for kind in HALO_ORDER for x in got[kind]]

    part_b, m1, m2, mf, mb = pl.pallas_call(
        functools.partial(second_kernel, geo=geo, skip=split),
        out_shape=[
            jax.ShapeDtypeStruct(((npair - 1 - split) * pitch, 2 * chans), F32),
            jax.ShapeDtypeStruct((2 * chans, (TALL - 2) * chans), BF16),
            mat, mat, mat,
        ],
        in_specs=[vmem] * 6,
        out_specs=[vmem] * 5,
        compiler_params=pltpu.CompilerParams(vmem_limit_bytes=16 * 2**20),
        cost_estimate=pl.CostEstimate(
            flops=work * (npair - 1 - split), bytes_accessed=8 * 2**20, transcendentals=0),
        name="noisy_second",
    )(pairs, mn, jnp.swapaxes(enc_w1, 1, 2), enc_w2, den_wa, den_wb)
    mats = [m1, m2, mn, mf, mb]

    flat = BASE + (npair + 3) * pitch + 16
    windows = geo["windows"]
    field_scratch = pltpu.VMEM((flat, 2 * chans), BF16)
    edge_scratch = pltpu.VMEM((BASE + 2 * pitch + 16, 2 * chans), BF16)
    cond_scratch = pltpu.VMEM(((TALL - 2) * cin * (windows - 1) + chans, cols), F32)
    whole_scratch = pltpu.VMEM((chans, rows, cols), BF16)
    inputs = [part_a, part_b, pairs, pairs, left, right, subs[0], *halos, *mats,
              enc_b1[None], enc_b2[None], den_ba[None], noise_gain[None]]
    in_specs = [vmem] * len(inputs)
    in_specs[2] = pl.BlockSpec((2 * pitch, 2 * chans), lambda i: (0, 0))
    in_specs[3] = pl.BlockSpec((2 * pitch, 2 * chans), lambda i: (last, 0))
    result = pl.pallas_call(
        functools.partial(main_kernel, geo=geo, n_strip_in=n_strip_out, n_sub_in=n_sub_out),
        grid=(1,),
        out_shape=jax.ShapeDtypeStruct((chans, rows, cols), BF16),
        in_specs=[vmem, vmem] + in_specs,
        out_specs=any_spec,
        scratch_shapes=[
            field_scratch, field_scratch, field_scratch,
            edge_scratch, edge_scratch,
            pltpu.VMEM((8 * npair + 16, 2 * chans), BF16),
            pltpu.VMEM((8 * (npair - 1), 2 * chans), F32),
            cond_scratch, cond_scratch,
            pltpu.VMEM((BASE + windows * pitch + 16, chans), F32),
            whole_scratch,
            pltpu.VMEM((chans * OUT_STRIDE, cols), F32),
            pltpu.SemaphoreType.DMA((-(-npair // 8),)),
        ],
        compiler_params=pltpu.CompilerParams(vmem_limit_bytes=28 * 2**20),
        name="denoise",
    )(scales, field, *inputs)
    return result[None]


def solution(mesh):
    return jax.shard_map(
        local,
        mesh=mesh,
        in_specs=(
            P(("group", "member"), None, "strip", "sub"),
            P("group", ("strip", "member"), "sub"),
            P(("group", "member")),
            P(),
            P(),
            P(),
            P(),
            P(),
            P(),
            P(),
            P(),
        ),
        out_specs=P(("group", "member"), None, "strip", "sub"),
        check_vma=False,
    )
```

```python
import functools
import math

import jax
import jax.numpy as jnp
from jax import lax
from jax.experimental import pallas as pl
from jax.experimental.pallas import tpu as pltpu
from jax.sharding import PartitionSpec as P

LEVELS = 18
SIGMA_DATA = 0.5
SIG_LOW = 0.25
SIG_HIGH = 4.0

BF16 = jnp.bfloat16
F32 = jnp.float32
NT = (((1,), (1,)), ((), ()))
NN = (((1,), (0,)), ((), ()))

BASE = 8
HALO = 4
EDGE = HALO
EARLY = 4
GROUP = 8
OUT_STRIDE = 17
HALO_ORDER = ("strip", "diag", "sub")
TALL = 6


def plan(level_ref):
    level = level_ref[0:1, :]
    sigma = SIG_LOW * jnp.exp(level * (math.log(SIG_HIGH / SIG_LOW) / (LEVELS - 1)))
    spread = sigma * sigma + SIGMA_DATA * SIGMA_DATA
    root = jnp.sqrt(spread)
    return 1.0 / root, SIGMA_DATA * SIGMA_DATA / spread, sigma * SIGMA_DATA / root, jnp.log(sigma) / 4.0


def prep_kernel(level_ref, field_hbm, cond_hbm, pairs_ref, left_ref, right_ref, cond_ref, scale_ref,
                raw, buf, sems, *, pitch):
    steps, chans, tall, cols = raw.shape
    gets = []
    for s in range(steps):
        get = pltpu.make_async_copy(field_hbm.at[:, pl.ds(s * tall, tall), :], raw.at[s], sems.at[s])
        get.start()
        gets.append(get)
    get_cond = pltpu.make_async_copy(cond_hbm, cond_ref, sems.at[steps])
    get_cond.start()
    c_in, c_skip, c_out, c_noise = plan(level_ref)
    scale_ref[...] = jnp.concatenate(
        [c_skip, c_out, c_noise, jnp.zeros((5, 128), F32)], axis=0)
    for s in range(steps):
        gets[s].wait()
        buf[...] = raw[s].astype(F32).reshape(chans * tall, cols)
        for q in range(tall // 2):
            at = s * (tall // 2) + q
            for h in range(2):
                row = buf[pl.ds(2 * q + h, chans, stride=tall), :]
                cells = (c_in * row.T).astype(BF16)
                lanes = slice(h * chans, (h + 1) * chans)
                pairs_ref[at * pitch + 2:at * pitch + 2 + cols, lanes] = cells
                left_ref[2 * at:2 * at + 2, lanes] = cells[:2]
                right_ref[2 * at:2 * at + 2, lanes] = cells[cols - 2:]
    get_cond.wait()


def pack_kernel(*refs, geo, order):
    block_count = len(order)
    top_ref, bottom_ref, left_ref, right_ref = refs[:4]
    blocks = [refs[4 + order.index(k)] for k in range(block_count)]
    outs = list(refs[4 + block_count + 1:])
    n_strip, n_sub, n_member = geo["n_strip"], geo["n_sub"], geo["n_member"]
    pitch, cols, rows, cin = geo["pitch"], geo["cols"], geo["rows"], geo["cin"]
    half = cin // 2
    member = lax.axis_index("member")
    strip = lax.axis_index("strip")
    sub = lax.axis_index("sub")

    n_sub_out = 1 if n_sub == 2 else 2
    rest, subs = outs[:-n_sub_out], outs[-n_sub_out:]
    whole = subs[0]
    for k, block in enumerate(blocks):
        tall = block.shape[1]
        if block_count == 1:
            at = 0
        else:
            at = pl.multiple_of(jnp.bitwise_xor(member, k) * tall, tall)
        for c in range(cin):
            lanes = slice((c // half) * cols, (c // half + 1) * cols)
            start = 2 * (rows // 2) + (c % half) * rows + at
            if block_count != 1:
                start = pl.multiple_of(start, 16)
            whole[pl.ds(start, tall), lanes] = block[c]
    noisy_rows = 2 * (rows // 2)
    whole_left = left_ref[...]
    whole_right = right_ref[...]

    def cond_edge(c, top):
        lanes = slice((c // half) * cols, (c // half + 1) * cols)
        start = noisy_rows + (c % half) * rows
        if top:
            return whole[start:start + EDGE, lanes]
        return whole[start + rows - EDGE:start + rows, lanes]

    def pick(flag, a, b):
        return jnp.where(flag, a.astype(F32), b.astype(F32)).astype(BF16)

    def pair_edge(top):
        if top:
            return top_ref[2:2 + cols, :]
        return bottom_ref[pitch + 2:pitch + 2 + cols, :]

    if n_sub == 2:
        whole[:noisy_rows, :] = pick(sub == 0, whole_right, whole_left)
    else:
        whole[:noisy_rows, :] = whole_left
        other = subs[1]
        other[noisy_rows:, :] = whole[noisy_rows:, :]
        other[:noisy_rows, :] = whole_right
    tops = [None] if n_strip == 2 else [True, False]
    for at, top in enumerate(tops):
        if top is None:
            pair = pick(strip == 0, pair_edge(False), pair_edge(True))
        else:
            pair = pair_edge(top)
        strip_out = rest[at]
        strip_out[:cols, :] = pair
        for c in range(cin):
            lanes = slice((c // half) * cols, (c // half + 1) * cols)
            if top is None:
                cells = pick(strip == 0, cond_edge(c, False), cond_edge(c, True))
            else:
                cells = cond_edge(c, top)
            start = cols + (c % half) * EDGE
            strip_out[start:start + EDGE, lanes] = cells


def corner_kernel(strip_ref, *outs, cols):
    cond_rows = strip_ref.shape[0] - cols
    for out in outs:
        out[:cond_rows, :] = strip_ref[cols:, :]
    if len(outs) == 1:
        first = lax.axis_index("sub") == 0
        cells = jnp.where(first, strip_ref[cols - 2:cols, :].astype(F32), strip_ref[:2, :].astype(F32))
        outs[0][cond_rows:cond_rows + 2, :] = cells.astype(BF16)
    else:
        outs[0][cond_rows:cond_rows + 2, :] = strip_ref[:2, :]
        outs[1][cond_rows:cond_rows + 2, :] = strip_ref[cols - 2:cols, :]


def conv(pieces, weight):
    lo, hi = slice(0, 128), slice(128, 256)

    def rows_of(lanes, shift, extra):
        return jnp.concatenate(
            [src[at + shift(pitch):at + shift(pitch) + span + extra, lanes]
             for src, at, span, pitch in pieces], axis=0)

    inner = []
    for b in range(3):
        inner.append(rows_of(hi, lambda pitch: b, 0))
        inner.append(rows_of(lo, lambda pitch: pitch + b, 0))
    y = lax.dot_general(
        jnp.concatenate(inner, axis=1), weight[:, :768], NT, preferred_element_type=F32)
    upper = jnp.concatenate([rows_of(lo, lambda pitch: b, 8) for b in range(2)], axis=1)
    upper = lax.dot_general(upper, weight[:, 768:1024], NT, preferred_element_type=F32)
    lower = jnp.concatenate([rows_of(hi, lambda pitch: pitch + b, 8) for b in range(2)], axis=1)
    lower = lax.dot_general(lower, weight[:, 1024:], NT, preferred_element_type=F32)
    results = []
    at = more = 0
    for _, _, span, _ in pieces:
        a, b = upper[more:more + span + 8], lower[more:more + span + 8]
        outer = [a[:span, lo] + a[1:span + 1, hi], b[:span, lo] + b[1:span + 1, hi]]
        results.append(y[at:at + span] + jnp.concatenate(outer, axis=1))
        at += span
        more += span + 8
    return results


def tiles_of(dst, src, lanes):
    zero = jnp.zeros((128, 128), BF16)
    tap = [[src[3 * a + b, :, lanes] for b in range(3)] for a in range(3)]

    def put(at, blocks):
        for n in range(2):
            for k in range(2):
                dst[n * 128:(n + 1) * 128, at + k * 128:at + (k + 1) * 128] = blocks[n][k]

    for b in range(3):
        put(b * 256, [[tap[1][b], tap[2][b]], [tap[0][b], tap[1][b]]])
    put(768, [[tap[0][0], tap[0][1]], [zero, tap[0][2]]])
    put(1024, [[tap[2][0], tap[2][1]], [zero, tap[2][2]]])


def chunks(total, size):
    return [(at, min(size, total - at)) for at in range(0, total, size)]


def first_kernel(pairs, wa, part, mn, *, pitch):
    tiles_of(mn, wa, slice(0, 128))
    for first, count in chunks(part.shape[0] // pitch, GROUP):
        part[first * pitch:(first + count) * pitch, :] = conv(
            [(pairs, first * pitch, count * pitch, pitch)], mn)[0]


def second_kernel(pairs, mn, w1, w2, wa, wb, part, m1, m2, mf, mb, *, geo, skip):
    pitch, cin = geo["pitch"], geo["cin"]
    chans = 128
    for first, count in chunks(part.shape[0] // pitch, GROUP):
        part[first * pitch:(first + count) * pitch, :] = conv(
            [(pairs, (skip + first) * pitch, count * pitch, pitch)], mn)[0]
    tiles_of(m2, w2, slice(0, chans))
    tiles_of(mf, wa, slice(chans, 2 * chans))
    tiles_of(mb, wb, slice(0, chans))
    m1[...] = jnp.zeros_like(m1)
    for b in range(3):
        for n in range(TALL - 2):
            for a in range(3):
                at = (b * TALL + n + a) * cin
                m1[at:at + cin, n * chans:(n + 1) * chans] = w1[3 * a + b]


def main_kernel(*refs, geo, n_strip_in, n_sub_in):
    it = iter(refs)
    scales = next(it)
    field = next(it)
    part_a, part_b, pairs_top, pairs_bottom, left, right, own = [next(it) for _ in range(7)]
    split = part_a.shape[0] // geo["pitch"]
    got = {}
    for kind in HALO_ORDER:
        count = dict(strip=n_strip_in, sub=n_sub_in, diag=n_strip_in * n_sub_in)[kind]
        got[kind] = [next(it) for _ in range(count)]
    strip_in, sub_in = got["strip"], got["sub"]
    diag_in = [got["diag"][k * n_sub_in:(k + 1) * n_sub_in] for k in range(n_strip_in)]
    m1, m2, mn, mf, mb, b1, b2, ba, gain = [next(it) for _ in range(9)]
    out_hbm = next(it)
    (xe, xf, xh, xt, xb, xc, yc, cr, ch, lw, out, obuf, sems) = list(it)

    n_strip, n_sub = geo["n_strip"], geo["n_sub"]
    pitch, cols, rows, cin = geo["pitch"], geo["cols"], geo["rows"], geo["cin"]
    chans = 128
    half = cin // 2
    npair = rows // 2
    noisy_rows = 2 * npair
    strip = lax.axis_index("strip")
    sub = lax.axis_index("sub")
    above, below = strip > 0, strip < n_strip - 1
    before, after = sub > 0, sub < n_sub - 1

    c_skip, c_out, c_noise = scales[0:1, :], scales[1:2, :], scales[2:3, :]

    def keep(flag, cells):
        return jnp.where(flag, cells.astype(F32), 0.0)

    strip_top, strip_bottom = strip_in[0], strip_in[-1]
    diag_top, diag_bottom = diag_in[0], diag_in[-1]

    def halo_cells(q):
        return (keep(before, sub_in[0][2 * q:2 * q + 2, :]).astype(BF16),
                keep(after, sub_in[-1][2 * q:2 * q + 2, :]).astype(BF16))

    corner = slice(half * EDGE, half * EDGE + 2)
    strip_rows = (
        (xt, strip_top, diag_top, above, 0, pairs_top[:pitch, :], 0, 1),
        (xb, strip_bottom, diag_bottom, below, 1, pairs_bottom[pitch:, :], npair - 1, 0))
    for dst, source, corners, flag, at, inner, q, inner_at in strip_rows:
        at = BASE + at * pitch
        dst[at + 2:at + 2 + cols, :] = keep(flag, source[:cols, :]).astype(BF16)
        dst[at:at + 2, :] = keep(flag & before, corners[0][corner, :]).astype(BF16)
        dst[at + 2 + cols:at + 4 + cols, :] = keep(flag & after, corners[-1][corner, :]).astype(BF16)
        at = BASE + inner_at * pitch
        dst[at:at + pitch, :] = inner
        dst[at:at + 2, :], dst[at + 2 + cols:at + 4 + cols, :] = halo_cells(q)
    for q in range(npair):
        at = 8 * q
        xc[at:at + 2, :], xc[at + 6:at + 8, :] = halo_cells(q)
        xc[at + 2:at + 4, :] = left[2 * q:2 * q + 2, :]
        xc[at + 4:at + 6, :] = right[2 * q:2 * q + 2, :]
    edge_top, edge_bottom, edge_cols = conv(
        [(xt, BASE, pitch, pitch), (xb, BASE, pitch, pitch), (xc, 0, 8 * (npair - 1), 8)], mn)
    yc[...] = edge_cols

    cr[...] = jnp.zeros_like(cr)
    ch[...] = jnp.zeros_like(ch)

    def lanes_of(c):
        return slice((c // half) * cols, (c // half + 1) * cols)

    def fill(dst, body, tops):
        for c in range(cin):
            at = noisy_rows + (c % half) * rows
            dst[pl.ds(HALO * cin + c, rows, stride=cin), :] = (
                body[at:at + rows, lanes_of(c)].astype(F32))
            for source, flag, is_top, first in tops:
                at = first + (c % half) * EDGE
                cells = source[at:at + EDGE, lanes_of(c)].astype(F32)
                if is_top:
                    dst[pl.ds(c, HALO, stride=cin), :] = keep(flag, cells[EDGE - HALO:])
                else:
                    dst[pl.ds((HALO + rows) * cin + c, HALO, stride=cin), :] = keep(flag, cells[:HALO])

    fill(cr, own, [(strip_top, above, True, cols), (strip_bottom, below, False, cols)])
    windows = geo["windows"]
    step = (TALL - 2) * cin
    for w in range(windows):
        at = BASE - HALO + w * pitch
        lw[at + HALO:at + HALO + cols, :] = cr[step * w:step * w + chans, :].T
    for k in range(n_sub_in):
        fill(ch, sub_in[k], [(diag_top[k], above, True, 0), (diag_bottom[k], below, False, 0)])
        for w in range(windows):
            cells = ch[step * w:step * w + chans, :].T
            at = BASE - HALO + w * pitch
            if k == 0:
                lw[at:at + HALO, :] = keep(before, cells[cols - HALO:])
            if k == n_sub_in - 1:
                lw[at + HALO + cols:at + 2 * HALO + cols, :] = keep(after, cells[:HALO])

    def inside(y, left, right, first, count, low_row):
        y = y.reshape(count, pitch, 2 * chans)
        col = lax.broadcasted_iota(jnp.int32, (count, 8, 2 * chans), 1)
        head = jnp.where((col >= left) | before, y[:, :8], 0.0)
        tail = jnp.where((col < right - (pitch - 8)) | after, y[:, pitch - 8:], 0.0)
        y = jnp.concatenate([head, y[:, 8:pitch - 8], tail], axis=1)
        parts = []
        for i in range(count):
            halves = []
            for h in range(2):
                row = 2 * (first + i) + h - low_row
                cells = y[i, :, h * chans:(h + 1) * chans]
                if row < 0:
                    cells = jnp.where(above, cells, 0.0)
                elif row >= rows:
                    cells = jnp.where(below, cells, 0.0)
                halves.append(cells)
            parts.append(jnp.concatenate(halves, axis=1))
        return parts

    def silu(v):
        return v * jax.nn.sigmoid(v)

    def twice(v):
        return jnp.concatenate([v, v], axis=1)

    bias1 = twice(b1[...])
    wide = TALL * cin
    lane = lax.broadcasted_iota(jnp.int32, (1, chans), 1)
    per = 9
    for w0 in range(0, windows, per):
        count = min(per, windows - w0)
        span = count * pitch
        at = BASE - HALO + w0 * pitch
        middle = pltpu.roll(lw[at + 1:at + 1 + span, :], wide, 1)
        last = pltpu.roll(lw[at + 2:at + 2 + span, :], 2 * wide - chans, 1)
        lhs = jnp.concatenate(
            [jnp.where(lane < wide, lw[at:at + span, :], middle),
             jnp.where(lane < 2 * wide - chans, middle, last)], axis=1).astype(BF16)
        y = lax.dot_general(lhs, m1[...], NN, preferred_element_type=F32)
        for p in range((TALL - 2) // 2):
            z = silu(y[:, p * 2 * chans:(p + 1) * 2 * chans] + bias1)
            for i in range(count):
                j = (TALL - 2) // 2 * (w0 + i) + p
                if j < npair + 3:
                    cells = inside(z[i * pitch:(i + 1) * pitch], 3, 3 + cols, j, 1, 3)[0]
                    xe[BASE + j * pitch:BASE + (j + 1) * pitch, :] = cells.astype(BF16)

    bias2 = twice(b2[...])
    for first, count in chunks(npair + 2, GROUP):
        y = conv([(xe, BASE + first * pitch, count * pitch, pitch)], m2)[0] + bias2
        parts = inside(y, 2, 2 + cols, first, count, 2)
        for i, cells in enumerate(parts):
            at = BASE + (first + i) * pitch
            xf[at:at + pitch, :] = cells.astype(BF16)

    offset = twice(ba[...] + c_noise * gain[...])
    first_cols = lax.broadcasted_iota(jnp.int32, (8, 2 * chans), 0) < 2
    for first, count in chunks(npair + 1, GROUP):
        y = conv([(xf, BASE + first * pitch, count * pitch, pitch)], mf)[0] + offset
        noisy = []
        for j in range(first, first + count):
            if j == 0:
                noisy.append(edge_top)
            elif j == npair:
                noisy.append(edge_bottom)
            else:
                part, at = (part_a, j - 1) if j - 1 < split else (part_b, j - 1 - split)
                at *= pitch
                edge = yc[8 * (j - 1):8 * j, :]
                noisy.append(jnp.where(first_cols, edge, part[at:at + 8, :]))
                noisy.append(part[at + 8:at + cols, :])
                noisy.append(jnp.where(
                    first_cols, pltpu.roll(edge, 4, 0), part[at + cols:at + cols + 8, :]))
        y = y + jnp.concatenate(noisy, axis=0)
        parts = inside(silu(y), 1, 1 + cols, first, count, 1)
        for i, cells in enumerate(parts):
            at = BASE + (first + i) * pitch
            xh[at:at + pitch, :] = cells.astype(BF16)

    puts = []
    for first, count in chunks(npair, 8):
        y = conv([(xh, BASE + j * pitch, cols, pitch) for j in range(first, first + count)], mb)
        tall = 2 * count
        for i in range(count):
            for h in range(2):
                cells = y[i][:, h * chans:(h + 1) * chans]
                obuf[pl.ds(2 * i + h, chans, stride=OUT_STRIDE), :] = cells.T
        r0 = 2 * first
        for c in range(chans):
            update = obuf[c * OUT_STRIDE:c * OUT_STRIDE + tall, :]
            skip = field[c, r0:r0 + tall, :].astype(F32)
            out[c, r0:r0 + tall, :] = (c_skip * skip + c_out * update).astype(BF16)
        put = pltpu.make_async_copy(
            out.at[:, pl.ds(r0, tall), :], out_hbm.at[:, pl.ds(r0, tall), :],
            sems.at[first // 8])
        put.start()
        puts.append(put)
    for put in puts:
        put.wait()


def local(
    noisy, condition, levels, enc_w1, enc_b1, enc_w2, enc_b2, den_wa, den_ba, noise_gain, den_wb
):
    field = noisy[0]
    chans, rows, cols = field.shape
    cin = condition.shape[0]
    n_member = lax.axis_size("member")
    n_strip = lax.axis_size("strip")
    n_sub = lax.axis_size("sub")
    pitch = cols + 2 * HALO
    npair = rows // 2
    geo = dict(n_strip=n_strip, n_sub=n_sub, n_member=n_member, pitch=pitch, cols=cols, rows=rows,
               cin=cin, windows=-(-(rows + 6) // (TALL - 2)))

    if n_member in (1, 2, 4):
        blocks = [condition]
        for k in range(1, n_member):
            blocks.append(
                lax.ppermute(condition, "member", [(i, i ^ k) for i in range(n_member)]))
    else:
        blocks = [lax.all_gather(condition, "member", axis=1, tiled=True)]

    tall = 16
    steps = rows // tall
    any_spec = pl.BlockSpec(memory_space=pl.ANY)
    vmem = pl.BlockSpec(memory_space=pltpu.VMEM)
    pairs, left, right, own_cond, scales = pl.pallas_call(
        functools.partial(prep_kernel, pitch=pitch),
        out_shape=[
            jax.ShapeDtypeStruct((npair * pitch + 16, 2 * chans), BF16),
            jax.ShapeDtypeStruct((2 * npair, 2 * chans), BF16),
            jax.ShapeDtypeStruct((2 * npair, 2 * chans), BF16),
            jax.ShapeDtypeStruct(condition.shape, BF16),
            jax.ShapeDtypeStruct((8, 128), F32),
        ],
        in_specs=[vmem] + [pl.BlockSpec(memory_space=pltpu.HBM)] * 2,
        out_specs=[vmem] * 5,
        scratch_shapes=[
            pltpu.VMEM((steps, chans, tall, cols), BF16),
            pltpu.VMEM((chans * tall, cols), F32),
            pltpu.SemaphoreType.DMA((steps + 1,)),
        ],
        compiler_params=pltpu.CompilerParams(vmem_limit_bytes=12 * 2**20),
        cost_estimate=pl.CostEstimate(flops=0, bytes_accessed=16 * 2**20, transcendentals=0),
        name="prep",
    )(jnp.broadcast_to(levels.astype(F32)[:, None], (8, 128)), *[pltpu.with_memory_space_constraint(x, pltpu.HBM) for x in (field, condition)])
    if len(blocks) > 1:
        blocks[0] = own_cond

    mat = jax.ShapeDtypeStruct((2 * chans, 10 * chans), BF16)
    work = 2 * 9 * chans * chans * 2 * cols
    split = EARLY
    part_a, mn = pl.pallas_call(
        functools.partial(first_kernel, pitch=pitch),
        out_shape=[jax.ShapeDtypeStruct((split * pitch, 2 * chans), F32), mat],
        in_specs=[vmem] * 2,
        out_specs=[vmem] * 2,
        compiler_params=pltpu.CompilerParams(vmem_limit_bytes=16 * 2**20),
        cost_estimate=pl.CostEstimate(
            flops=work * split, bytes_accessed=4 * 2**20, transcendentals=0),
        name="noisy_first",
    )(pairs, den_wa)

    whole_shape = jax.ShapeDtypeStruct((2 * npair + cin // 2 * rows, 2 * cols), BF16)
    strip_shape = jax.ShapeDtypeStruct((cols + cin // 2 * EDGE, 2 * cols), BF16)
    diag_shape = jax.ShapeDtypeStruct((cin // 2 * EDGE + 8, 2 * cols), BF16)
    n_sub_out = 1 if n_sub == 2 else 2
    n_strip_out = 1 if n_strip == 2 else 2
    out_shape = [strip_shape] * n_strip_out + [whole_shape] * n_sub_out
    last = npair // 2 - 1
    order = sorted(range(len(blocks)), key=lambda k: (0, 3, 1, 2).index(k))
    packed = pl.pallas_call(
        functools.partial(pack_kernel, geo=geo, order=order),
        grid=(1,),
        out_shape=out_shape,
        in_specs=[
            pl.BlockSpec((2 * pitch, 2 * chans), lambda i: (0, 0)),
            pl.BlockSpec((2 * pitch, 2 * chans), lambda i: (last, 0)),
        ] + [vmem] * (2 + len(blocks)) + [any_spec],
        out_specs=[vmem] * len(out_shape),
        compiler_params=pltpu.CompilerParams(vmem_limit_bytes=8 * 2**20),
        name="pack",
    )(pairs, pairs, left, right, *[blocks[k] for k in order], part_a)

    def up(n):
        return [(i, i - 1) for i in range(1, n)]

    def down(n):
        return [(i, i + 1) for i in range(n - 1)]

    sub_moves = [up(n_sub) + down(n_sub)] if n_sub == 2 else [up(n_sub), down(n_sub)]
    strip_moves = [up(n_strip) + down(n_strip)] if n_strip == 2 else [up(n_strip), down(n_strip)]
    strips, subs = packed[:-n_sub_out], packed[-n_sub_out:]
    diags = [
        pl.pallas_call(
            functools.partial(corner_kernel, cols=cols),
            out_shape=[diag_shape] * n_sub_out,
            in_specs=[vmem],
            out_specs=[vmem] * n_sub_out,
            compiler_params=pltpu.CompilerParams(vmem_limit_bytes=8 * 2**20),
            name="corners",
        )(strip)
        for strip in strips
    ]
    sub_in = [lax.ppermute(x, "sub", move) for x, move in zip(subs, sub_moves)]
    diag_in = []
    for k, move in enumerate(strip_moves):
        corners = []
        for n, side in enumerate(sub_moves):
            pairs_of = [(i * n_sub + j, p * n_sub + q) for i, p in move for j, q in side]
            corners.append(lax.ppermute(diags[k][n], ("strip", "sub"), pairs_of))
        diag_in.append(corners[::-1])
    strip_in = [lax.ppermute(x, "strip", move) for x, move in zip(strips, strip_moves)]
    got = dict(strip=strip_in[::-1], sub=sub_in[::-1], diag=[x for y in diag_in[::-1] for x in y])
    halos = [x for kind in HALO_ORDER for x in got[kind]]

    part_b, m1, m2, mf, mb = pl.pallas_call(
        functools.partial(second_kernel, geo=geo, skip=split),
        out_shape=[
            jax.ShapeDtypeStruct(((npair - 1 - split) * pitch, 2 * chans), F32),
            jax.ShapeDtypeStruct((2 * chans, (TALL - 2) * chans), BF16),
            mat, mat, mat,
        ],
        in_specs=[vmem] * 6,
        out_specs=[vmem] * 5,
        compiler_params=pltpu.CompilerParams(vmem_limit_bytes=16 * 2**20),
        cost_estimate=pl.CostEstimate(
            flops=work * (npair - 1 - split), bytes_accessed=8 * 2**20, transcendentals=0),
        name="noisy_second",
    )(pairs, mn, jnp.swapaxes(enc_w1, 1, 2), enc_w2, den_wa, den_wb)
    mats = [m1, m2, mn, mf, mb]

    flat = BASE + (npair + 3) * pitch + 16
    windows = geo["windows"]
    field_scratch = pltpu.VMEM((flat, 2 * chans), BF16)
    edge_scratch = pltpu.VMEM((BASE + 2 * pitch + 16, 2 * chans), BF16)
    cond_scratch = pltpu.VMEM(((TALL - 2) * cin * (windows - 1) + chans, cols), F32)
    whole_scratch = pltpu.VMEM((chans, rows, cols), BF16)
    inputs = [part_a, part_b, pairs, pairs, left, right, subs[0], *halos, *mats,
              enc_b1[None], enc_b2[None], den_ba[None], noise_gain[None]]
    in_specs = [vmem] * len(inputs)
    in_specs[2] = pl.BlockSpec((2 * pitch, 2 * chans), lambda i: (0, 0))
    in_specs[3] = pl.BlockSpec((2 * pitch, 2 * chans), lambda i: (last, 0))
    result = pl.pallas_call(
        functools.partial(main_kernel, geo=geo, n_strip_in=n_strip_out, n_sub_in=n_sub_out),
        grid=(1,),
        out_shape=jax.ShapeDtypeStruct((chans, rows, cols), BF16),
        in_specs=[vmem, vmem] + in_specs,
        out_specs=any_spec,
        scratch_shapes=[
            field_scratch, field_scratch, field_scratch,
            edge_scratch, edge_scratch,
            pltpu.VMEM((8 * npair + 16, 2 * chans), BF16),
            pltpu.VMEM((8 * (npair - 1), 2 * chans), F32),
            cond_scratch, cond_scratch,
            pltpu.VMEM((BASE + windows * pitch + 16, chans), F32),
            whole_scratch,
            pltpu.VMEM((chans * OUT_STRIDE, cols), F32),
            pltpu.SemaphoreType.DMA((-(-npair // 8),)),
        ],
        compiler_params=pltpu.CompilerParams(vmem_limit_bytes=28 * 2**20),
        name="denoise",
    )(scales, field, *inputs)
    return result[None]


def solution(mesh):
    return jax.shard_map(
        local,
        mesh=mesh,
        in_specs=(
            P(("group", "member"), None, "strip", "sub"),
            P("group", ("strip", "member"), "sub"),
            P(("group", "member")),
            P(),
            P(),
            P(),
            P(),
            P(),
            P(),
            P(),
            P(),
        ),
        out_specs=P(("group", "member"), None, "strip", "sub"),
        check_vma=False,
    )
```
